256 devices in a mesh: slab: 64 (over y, z, core), grp: 4 (over x).
Axes of the slice: x: 4, y: 4, z: 8, core: 2. Of those that a mesh axis runs over, the one named last changes fastest.
Arguments:
- surf_pos: float32 [3, 1048576], P(None, ('slab', 'grp')), may hold values from -1 to 1
- surf_motion: float32 [7, 1048576], P(None, ('slab', 'grp')), may hold values from -6 to 6
- surf_bin: int32 [1048576], P(('slab', 'grp')), may hold values from 0 to 255, as said below
- vol_pos: float32 [3, 262144], P(None, ('slab', 'grp')), may hold values from -1 to 1
- influence: int32 [256, 8], P(('slab', 'grp')), may hold values from 0 to 255, as said below
- list_count: int32 [256], P(('slab', 'grp')), may hold values from 2 to 8
Outputs:
- vol_motion: float32 [7, 262144], P(None, ('slab', 'grp'))
The draws below stay inside these ranges and needn't reach their ends.
Inputs may be any that keep to these rules, and one draw needn't show every extreme that they name: `surf_bin`: A node on the device at place d = s * 4 + g of the slab+grp order has a bin of the form t * 4 + g; each device gives exactly 64 of its nodes to each slab t, so every bin holds 4096 nodes. `influence`: row d = s * 4 + g holds 8 distinct bin ids b with |b // 4 - s| <= 2; only the first list_count[d] are used.
All inputs are finite; a program needn't handle non-finite values.
Results may differ from the reference program's by a relative error of at most 0.0003.
Values sent between devices are 32-bit elements; how exact they have to be, the bound alone decides.
A program may use at most 128 MiB of HBM per device.

```python
import jax
import jax.numpy as jnp
from jax import lax

BIN = 4096
VOL_DEV = 1024
LMAX = 8
REACH = 2
NBINS = 256
SURF = 1048576
VOL = 262144
N_SLAB = 64
N_GRP = 4


def surface_places(key, lower, extent):
    return lower + extent * jax.random.uniform(key, (3, SURF), jnp.float32)


def draw_surf_pos(key, part):
    return surface_places(key, -1.0, 2.0)


def draw_surf_motion(key, part):
    key = jax.random.fold_in(key, 14)
    return jax.random.truncated_normal(key, -6.0, 6.0, (7, SURF), jnp.float32)


def draw_surf_bin(key, part):
    key = jax.random.fold_in(key, 11)
    keys = jax.random.split(key, NBINS)
    span = BIN // N_SLAB

    def one_device(device_key):
        return jax.random.permutation(device_key, BIN) // span
    target = jax.vmap(one_device)(keys)
    grp_of = (jnp.arange(NBINS) % N_GRP)[:, None]
    return (target * N_GRP + grp_of).reshape(-1).astype(jnp.int32)


def draw_influence(key, part):
    key = jax.random.fold_in(key, 12)
    cands = (2 * REACH + 1) * N_GRP
    slab_of = (jnp.arange(NBINS) // N_GRP)[:, None]
    column = jnp.arange(cands)[None, :]
    cand_slab = slab_of - REACH + column // N_GRP
    cand_bin = cand_slab * N_GRP + column % N_GRP
    inside = (cand_slab >= 0) & (cand_slab < N_SLAB)
    scores = jax.random.randint(key, (NBINS, cands), 0, 1 << 20) * 64 + column
    scores = jnp.where(inside, scores, -1 - column)
    picked = jax.lax.top_k(scores, LMAX)[1]
    return jnp.take_along_axis(cand_bin, picked, axis=1).astype(jnp.int32)


def draw_list_count(key, part):
    key = jax.random.fold_in(key, 13)
    first, second = jax.random.split(key)
    counts = jax.random.randint(first, (NBINS,), 2, LMAX + 1)
    place = jax.random.randint(second, (), 0, NBINS)
    return counts.at[place].set(LMAX).astype(jnp.int32)


def levels(rng, shape, cuts, low, top_value):
    def one(axis_at, shards_of):
        heights = jax.random.uniform(jax.random.fold_in(jax.random.fold_in(rng, 6), axis_at), (shards_of,), jnp.float32, low / len(cuts), top_value / len(cuts))
        return jnp.repeat(jnp.exp(heights), shape[axis_at] // shards_of).reshape((-1,) + (1,) * (len(shape) - axis_at - 1))

    loudness = one(*cuts[0])
    for cut in cuts[1:]:
        loudness = loudness * one(*cut)
    return loudness


def setup_inputs(seed: int = 0) -> dict:
    key_list = jax.random.split(jax.random.key(seed), 7)
    return {
        "surf_pos": draw_surf_pos(jax.random.fold_in(key_list[6], 71), 0),
        "surf_motion": draw_surf_motion(jax.random.fold_in(key_list[6], 71), 0),
        "surf_bin": draw_surf_bin(jax.random.fold_in(key_list[6], 71), 0),
        "vol_pos": jnp.clip(jax.random.uniform(key_list[3], (3, VOL), jnp.float32, -1.0, 1.0) * levels(key_list[3], (3, VOL), ((1, 256),), -0.4, 0.0), -1.0, 1.0),
        "influence": draw_influence(jax.random.fold_in(key_list[6], 71), 0),
        "list_count": draw_list_count(jax.random.fold_in(key_list[6], 71), 0),
    }


def blend_rows(vol, pos, mot):
    r2 = (vol[0][:, None] - pos[0][None, :]) ** 2
    r2 = r2 + (vol[1][:, None] - pos[1][None, :]) ** 2
    r2 = r2 + (vol[2][:, None] - pos[2][None, :]) ** 2
    inverse = 1.0 / (r2 + 0.01)
    weight = inverse * inverse
    numer = jnp.einsum("cb,vb->cv", mot, weight, precision=lax.Precision.HIGHEST)
    return numer, jnp.sum(weight, axis=1)


def blend(vol, pos, mot):
    count = vol.shape[1]
    rows = min(512, count)
    blocks = count // rows
    pieces = vol.reshape(3, blocks, rows).transpose(1, 0, 2)
    numer, denom = lax.map(lambda piece: blend_rows(piece, pos, mot), pieces)
    return numer.transpose(1, 0, 2).reshape(7, count), denom.reshape(count)


def reference(surf_pos, surf_motion, surf_bin, vol_pos, influence, list_count):
    order = jnp.argsort(surf_bin, stable=True)
    bin_pos = surf_pos[:, order].reshape(3, NBINS, BIN).transpose(1, 0, 2)
    bin_mot = surf_motion[:, order].reshape(7, NBINS, BIN).transpose(1, 0, 2)
    volumes = vol_pos.reshape(3, NBINS, VOL_DEV).transpose(1, 0, 2)

    def device(items):
        vol, row, count = items

        def step(index, carry):
            numer, denom = carry
            bin_id = row[index]
            extra_num, extra_den = blend(vol, bin_pos[bin_id], bin_mot[bin_id])
            return numer + extra_num, denom + extra_den

        start = (jnp.zeros((7, VOL_DEV), jnp.float32), jnp.zeros((VOL_DEV,), jnp.float32))
        numer, denom = lax.fori_loop(0, count, step, start)
        return numer / denom[None, :]

    result = lax.map(device, (volumes, influence, list_count))
    return result.transpose(1, 0, 2).reshape(7, NBINS * VOL_DEV)
```

```python
import functools

import jax
import jax.numpy as jnp
from jax import lax
from jax.experimental import pallas as pl
from jax.experimental.pallas import tpu as pltpu
from jax.sharding import PartitionSpec as P

F32, BF16 = jnp.float32, jnp.bfloat16
MESH = pl.DeviceIdType.MESH
VMEM = pl.BlockSpec(memory_space=pltpu.VMEM)
SMEM = pl.BlockSpec(memory_space=pltpu.SMEM)
ROWS = 16
LANES = 128
CORES = 2


def dot(a, b):
    return lax.dot_general(a, b, (((1,), (0,)), ((), ())), preferred_element_type=F32)


def split3(x):
    first = x.astype(BF16).astype(F32)
    rest = x - first
    second = rest.astype(BF16).astype(F32)
    return first, second, (rest - second).astype(BF16).astype(F32)


def place():
    slab = lax.axis_index("slab")
    return slab // CORES, slab % CORES, lax.axis_index("grp")


def peer_of(me, offset, ngrp):
    other = (me + offset) % (CORES * ngrp)
    return other // ngrp, other % ngrp


def exchange_kernel(nchip, ngrp, pos, mot, bins, vol, infl, cnt, win, vols, lists,
                    xs, dcol, send, a_send, a_recv, f_send, f_recv, v_send, v_recv, l_send, l_recv):
    q, c, x = place()
    nz = nchip // ngrp
    blocks = bins.shape[0]
    nslab = nchip * CORES
    span = LANES // CORES
    members = CORES * ngrp
    me = c * ngrp + x
    up, down = (q + 1) % nchip, (q + nchip - 1) % nchip

    barrier = pltpu.get_barrier_semaphore()

    def greet(device):
        pl.semaphore_signal(barrier, inc=1, device_id=device, device_id_type=MESH)

    def greet_source(i, carry):
        greet((i * CORES + 1 - c, (x + ngrp - i // nz) % ngrp))
        return carry

    lax.fori_loop(0, nchip, greet_source, 0)
    greet((up * CORES + c, x))
    greet((down * CORES + c, x))
    for o in range(1, members):
        pc, px = peer_of(me, o, ngrp)
        greet((q * CORES + pc, px))

    vols[pl.ds(me, 1)] = vol[...][None]
    lane = lax.broadcasted_iota(jnp.int32, (1, LANES), 1)
    row = jnp.where(lane == infl.shape[1], cnt[0], 0)
    for l in range(infl.shape[1]):
        row = jnp.where(lane == l, infl[0, l], row)
    lists[pl.ds(me, 1)] = row[None]

    xs[...] = jnp.zeros_like(xs)
    xs[0:7, :] = mot[...]
    xs[8:11, :] = pos[...]
    slab_of = bins[...] // ngrp
    sub = lax.broadcasted_iota(jnp.int32, (nslab, LANES), 0)
    tri_r = lax.broadcasted_iota(jnp.int32, (LANES, 2 * LANES), 0)
    tri_c = lax.broadcasted_iota(jnp.int32, (LANES, 2 * LANES), 1)
    tri = jnp.where((tri_r <= tri_c), 1.0, 0.0).astype(BF16)
    carry = jnp.zeros((nslab, LANES), F32)
    for k in range(blocks):
        trow = slab_of[k : k + 1, :]
        hit = trow == sub
        cum = dot(jnp.where(hit, 1.0, 0.0).astype(BF16), tri)
        rank = jnp.sum(jnp.where(hit, cum[:, :LANES] + carry, 0.0), axis=0, keepdims=True)
        carry = carry + cum[:, LANES:]
        dest = trow.astype(F32) * span + (rank - 1.0)
        wide = jnp.broadcast_to(dest, (LANES, LANES)).T
        dcol[k * LANES : (k + 1) * LANES, :] = wide.astype(jnp.int32)

    pl.semaphore_wait(barrier, nchip + 2 + members - 1)

    for o in range(1, members):
        pc, px = peer_of(me, o, ngrp)
        pltpu.make_async_remote_copy(
            src_ref=vols.at[me], dst_ref=vols.at[me], send_sem=v_send.at[o], recv_sem=v_recv.at[o],
            device_id=(q * CORES + pc, px), device_id_type=MESH).start()
        pltpu.make_async_remote_copy(
            src_ref=lists.at[me], dst_ref=lists.at[me], send_sem=l_send.at[o], recv_sem=l_recv.at[o],
            device_id=(q * CORES + pc, px), device_id_type=MESH).start()

    slot = x * nz + q % nz
    step_lanes = 2 * LANES
    steps = nchip // 2
    lane2 = lax.broadcasted_iota(jnp.int32, (step_lanes, LANES), 1)

    def to_bin(i):
        return pltpu.make_async_remote_copy(
            src_ref=send.at[i], dst_ref=win.at[1, slot], send_sem=a_send.at[i], recv_sem=a_recv.at[slot],
            device_id=(i * CORES + 1 - c, (x + q // nz) % ngrp), device_id_type=MESH)

    def order(i, _):
        tile = (q // 2 + i) % steps
        acc = jnp.zeros((3 * ROWS, step_lanes), F32)
        for k in range(blocks // 2):
            cols = slice(k * step_lanes, (k + 1) * step_lanes)
            part = jnp.concatenate(split3(xs[:, cols]), axis=0).astype(BF16)
            d = dcol[cols, :] - tile * step_lanes
            one = jnp.concatenate(
                [jnp.where(d == lane2, 1.0, 0.0), jnp.where(d == lane2 + LANES, 1.0, 0.0)], axis=1).astype(BF16)
            acc = acc + dot(part, one)
        full = acc[:ROWS] + acc[ROWS : 2 * ROWS] + acc[2 * ROWS :]
        send[2 * tile] = full[:, :LANES]
        send[2 * tile + 1] = full[:, LANES:]
        to_bin(2 * tile).start()
        to_bin(2 * tile + 1).start()
        return 0

    lax.fori_loop(0, steps, order, 0)

    def forward(g, to):
        part = pl.ds(g * nz, nz)
        return pltpu.make_async_remote_copy(
            src_ref=win.at[1, part], dst_ref=win.at[0 if to == 0 else 2, part],
            send_sem=f_send.at[to, g], recv_sem=f_recv.at[to, g],
            device_id=((up if to == 0 else down) * CORES + c, x), device_id_type=MESH)

    for g in range(ngrp):
        def arrived(z, _, g=g):
            s = g * nz + z
            pltpu.make_async_remote_copy(
                src_ref=send.at[0], dst_ref=win.at[1, s], send_sem=a_send.at[0], recv_sem=a_recv.at[s],
                device_id=(q * CORES + 1 - c, x), device_id_type=MESH).wait_recv()
            return 0

        lax.fori_loop(0, nz, arrived, 0)
        forward(g, 0).start()
        forward(g, 1).start()

    def left(i, _):
        to_bin(i).wait_send()
        return 0

    lax.fori_loop(0, nchip, left, 0)
    for o in range(1, members):
        other = (me + members - o) % members
        pc, px = peer_of(me, o, ngrp)
        for ref, s_sem, r_sem in ((vols, v_send, v_recv), (lists, l_send, l_recv)):
            copy = pltpu.make_async_remote_copy(
                src_ref=ref.at[me], dst_ref=ref.at[other], send_sem=s_sem.at[o], recv_sem=r_sem.at[o],
                device_id=(q * CORES + pc, px), device_id_type=MESH)
            copy.wait_send()
            copy.wait_recv()
    for g in range(ngrp):
        for to in range(2):
            copy = forward(g, to)
            copy.wait_send()
            copy.wait_recv()


def exchange(nchip, ngrp, pos, mot, bins, vol, infl, cnt):
    members = CORES * ngrp
    nvol = vol.shape[1]
    width = pos.shape[1]
    dma = pltpu.SemaphoreType.DMA
    return pl.pallas_call(
        functools.partial(exchange_kernel, nchip, ngrp),
        out_shape=(
            jax.ShapeDtypeStruct((3, nchip, ROWS, LANES), F32),
            jax.ShapeDtypeStruct((members, 3, nvol), F32),
            jax.ShapeDtypeStruct((members, 1, LANES), jnp.int32),
        ),
        in_specs=[VMEM, VMEM, VMEM, VMEM, SMEM, SMEM],
        out_specs=(VMEM, VMEM, VMEM),
        scratch_shapes=[
            pltpu.VMEM((ROWS, width), F32),
            pltpu.VMEM((width, LANES), jnp.int32),
            pltpu.VMEM((nchip, ROWS, LANES), F32),
            dma((nchip,)), dma((nchip,)),
            dma((2, ngrp)), dma((2, ngrp)),
            dma((members,)), dma((members,)),
            dma((members,)), dma((members,)),
        ],
        compiler_params=pltpu.CompilerParams(collective_id=0, has_side_effects=True, vmem_limit_bytes=48 << 20),
    )(pos, mot, bins, vol, infl, cnt)


def blend_kernel(ngrp, lists, win, vols, part, fs, mt, fv, acc):
    q, _, _ = place()
    members, _, nvol = vols.shape
    lmax_at = 8
    nz = win.shape[1] // ngrp
    base = (q - 1) * CORES * ngrp

    lane = lax.broadcasted_iota(jnp.int32, (ROWS, LANES), 1) < LANES // 2
    sub = lax.broadcasted_iota(jnp.int32, (8, LANES), 0)

    def features(t):
        first, second, third = split3(t)
        return first, second, third

    def prepare(i, _):
        chip, g = i // ngrp, i % ngrp
        for k in range(nz // 2):
            a = win[chip, g * nz + 2 * k]
            b = win[chip, g * nz + 2 * k + 1]
            pair = (jnp.where(lane, a, pltpu.roll(b, LANES // 2, 1)),
                    jnp.where(lane, pltpu.roll(a, LANES // 2, 1), b))
            cols = slice(k * LANES, (k + 1) * LANES)
            for tt in range(CORES):
                n = (chip * CORES + tt) * ngrp + g
                m = jnp.where(sub == 7, 1.0, pair[tt][:8])
                m1, m2, _ = split3(m)
                mt[n, :, cols] = jnp.concatenate([m1, m2], axis=0).astype(BF16)
                p = pair[tt][8:]
                p2 = p * p
                norm = p2[0:1] + p2[1:2] + p2[2:3] + 0.01
                y = jnp.where(sub < 3, -2.0 * p, jnp.where(sub == 3, norm, jnp.where(sub == 4, 1.0, 0.0)))
                y1, y2, y3 = split3(y)
                wide = jnp.concatenate([y1, y2, y3, y1, y2, y1], axis=0)
                fs[n, cols, :] = wide.T.astype(BF16)
        return 0

    lax.fori_loop(0, 3 * ngrp, prepare, 0)

    def prepare_vol(j, _):
        v = vols[j]
        v2 = v * v
        norm = v2[0:1] + v2[1:2] + v2[2:3]
        ones = jnp.ones_like(norm)
        zero = jnp.zeros_like(norm)
        w1, w2, w3 = split3(jnp.concatenate([v, ones, norm, zero, zero, zero], axis=0))
        fv[j] = jnp.concatenate([w1, w1, w1, w2, w2, w3], axis=0).astype(BF16)
        return 0

    lax.fori_loop(0, members, prepare_vol, 0)

    def block(j, _):
        acc[...] = jnp.zeros_like(acc)

        def item(l, _):
            n = lists[j, 0, l] - base
            d2 = dot(fs[n], fv[j])
            w = pltpu.reciprocal(d2 * d2, approx=True)
            w1 = w.astype(BF16)
            w2 = (w - w1.astype(F32)).astype(BF16)
            m = mt[n]
            acc[...] += dot(m, w1) + dot(m, w2)
            return 0

        lax.fori_loop(0, lists[j, 0, lmax_at], item, 0)
        part[j] = acc[:8] + acc[8:]
        return 0

    lax.fori_loop(0, members, block, 0)


def blend(ngrp, lists, win, vols):
    members, _, nvol = vols.shape
    nbin = 3 * CORES * ngrp
    nodes = win.shape[1] // ngrp * LANES // CORES
    return pl.pallas_call(
        functools.partial(blend_kernel, ngrp),
        out_shape=jax.ShapeDtypeStruct((members, 8, nvol), F32),
        in_specs=[SMEM, VMEM, VMEM],
        out_specs=VMEM,
        scratch_shapes=[
            pltpu.VMEM((nbin, nodes, 48), BF16),
            pltpu.VMEM((nbin, 16, nodes), BF16),
            pltpu.VMEM((members, 48, nvol), BF16),
            pltpu.VMEM((16, nvol), F32),
        ],
        compiler_params=pltpu.CompilerParams(vmem_limit_bytes=48 << 20),
    )(lists, win, vols)


def combine_kernel(ngrp, part, out, got, s_sem, r_sem):
    q, c, x = place()
    members = CORES * ngrp
    me = c * ngrp + x
    barrier = pltpu.get_barrier_semaphore()
    for o in range(1, members):
        pc, px = peer_of(me, o, ngrp)
        pl.semaphore_signal(barrier, inc=1, device_id=(q * CORES + pc, px), device_id_type=MESH)
    pl.semaphore_wait(barrier, members - 1)
    copies = []
    for o in range(1, members):
        pc, px = peer_of(me, o, ngrp)
        copy = pltpu.make_async_remote_copy(
            src_ref=part.at[(me + o) % members], dst_ref=got.at[o], send_sem=s_sem.at[o], recv_sem=r_sem.at[o],
            device_id=(q * CORES + pc, px), device_id_type=MESH)
        copy.start()
        copies.append(copy)
    total = part[me]
    for o in range(1, members):
        copies[o - 1].wait_recv()
        total = total + got[o]
    out[...] = total[:7] / total[7:8]
    for copy in copies:
        copy.wait_send()


def combine(ngrp, part):
    members, _, nvol = part.shape
    return pl.pallas_call(
        functools.partial(combine_kernel, ngrp),
        out_shape=jax.ShapeDtypeStruct((7, nvol), F32),
        in_specs=[VMEM],
        out_specs=VMEM,
        scratch_shapes=[
            pltpu.VMEM((members, 8, nvol), F32),
            pltpu.SemaphoreType.DMA((members,)),
            pltpu.SemaphoreType.DMA((members,)),
        ],
        compiler_params=pltpu.CompilerParams(collective_id=1, has_side_effects=True, vmem_limit_bytes=48 << 20),
    )(part)


def on_device(surf_pos, surf_motion, surf_bin, vol_pos, influence, list_count):
    nchip = lax.axis_size("slab") // CORES
    ngrp = lax.axis_size("grp")
    bins = surf_bin.reshape(-1, LANES)
    win, vols, lists = exchange(nchip, ngrp, surf_pos, surf_motion, bins, vol_pos, influence, list_count)
    part = blend(ngrp, lists, win, vols)
    return combine(ngrp, part)


def solution(mesh):
    return jax.shard_map(
        on_device,
        mesh=mesh,
        in_specs=(
            P(None, ("slab", "grp")),
            P(None, ("slab", "grp")),
            P(("slab", "grp")),
            P(None, ("slab", "grp")),
            P(("slab", "grp"), None),
            P(("slab", "grp")),
        ),
        out_specs=P(None, ("slab", "grp")),
        check_vma=False,
    )
```

```python
import functools

import jax
import jax.numpy as jnp
from jax import lax
from jax.experimental import pallas as pl
from jax.experimental.pallas import tpu as pltpu
from jax.sharding import PartitionSpec as P

F32, BF16 = jnp.float32, jnp.bfloat16
MESH = pl.DeviceIdType.MESH
VMEM = pl.BlockSpec(memory_space=pltpu.VMEM)
SMEM = pl.BlockSpec(memory_space=pltpu.SMEM)
HBM = pl.BlockSpec(memory_space=pltpu.HBM)
ROWS = 10
LANES = 128
CORES = 2
DEPTH = 48


def dot(a, b, dims=((1,), (0,))):
    return lax.dot_general(a, b, (dims, ((), ())), preferred_element_type=F32)


def split3(x):
    first = x.astype(BF16).astype(F32)
    rest = x - first
    second = rest.astype(BF16).astype(F32)
    return first, second, (rest - second).astype(BF16).astype(F32)


def place():
    slab = lax.axis_index("slab")
    return slab // CORES, slab % CORES, lax.axis_index("grp")


def peer_of(me, offset, ngrp):
    other = (me + offset) % (CORES * ngrp)
    return other // ngrp, other % ngrp


def exchange_kernel(nchip, ngrp, pos_in, mot_in, bins_in, vol_in, infl, cnt, fs, mt, fv, lists,
                    pos, mot, bins, vols, xp, dcol, send, win,
                    in_sem, a_send, a_recv, f_send, f_recv, v_send, v_recv, l_send, l_recv):
    q, c, x = place()
    nz = nchip // ngrp
    blocks = bins.shape[0]
    nslab = nchip * CORES
    span = LANES // CORES
    members = CORES * ngrp
    me = c * ngrp + x
    up, down = (q + 1) % nchip, (q + nchip - 1) % nchip

    loads = [pltpu.make_async_copy(bins_in, bins, in_sem.at[0]), pltpu.make_async_copy(mot_in, mot, in_sem.at[1]),
             pltpu.make_async_copy(pos_in, pos, in_sem.at[2]), pltpu.make_async_copy(vol_in, vols.at[me], in_sem.at[3])]
    for load in loads:
        load.start()

    barrier = pltpu.get_barrier_semaphore()

    def greet(device):
        pl.semaphore_signal(barrier, inc=1, device_id=device, device_id_type=MESH)

    def greet_source(i, carry):
        greet((i * CORES + 1 - c, (x + ngrp - i // nz) % ngrp))
        return carry

    lax.fori_loop(0, nchip, greet_source, 0)
    greet((up * CORES + c, x))
    greet((down * CORES + c, x))
    for o in range(1, members):
        pc, px = peer_of(me, o, ngrp)
        greet((q * CORES + pc, px))

    lane = lax.broadcasted_iota(jnp.int32, (1, LANES), 1)
    row = jnp.where(lane == infl.shape[1], cnt[0], 0)
    for l in range(infl.shape[1]):
        row = jnp.where(lane == l, infl[0, l], row)
    lists[pl.ds(me, 1)] = row[None]

    loads[0].wait()
    slab_of = bins[...] // ngrp
    sub = lax.broadcasted_iota(jnp.int32, (nslab, LANES), 0)
    tri_r = lax.broadcasted_iota(jnp.int32, (LANES, 2 * LANES), 0)
    tri_c = lax.broadcasted_iota(jnp.int32, (LANES, 2 * LANES), 1)
    tri = jnp.where((tri_r <= tri_c), 1.0, 0.0).astype(BF16)
    carry = jnp.zeros((nslab, LANES), F32)
    for k in range(blocks):
        trow = slab_of[k : k + 1, :]
        hit = trow == sub
        cum = dot(jnp.where(hit, 1.0, 0.0).astype(BF16), tri)
        rank = jnp.sum(jnp.where(hit, cum[:, :LANES] + carry, 0.0), axis=0, keepdims=True)
        carry = carry + cum[:, LANES:]
        dest = trow.astype(F32) * span + (rank - 1.0)
        wide = jnp.broadcast_to(dest, (LANES, LANES)).T
        dcol[k * LANES : (k + 1) * LANES, :] = wide.astype(jnp.int32)

    for load in loads[1:]:
        load.wait()
    whole = jnp.concatenate([mot[...], pos[...], jnp.zeros((16 - ROWS, mot.shape[1]), F32)], axis=0)
    xp[...] = jnp.concatenate(split3(whole), axis=0).astype(BF16)

    slot = x * nz + q % nz
    wide2 = 2 * LANES
    steps = nchip // 4
    lane2 = lax.broadcasted_iota(jnp.int32, (wide2, LANES), 1)

    def to_bin(i):
        return pltpu.make_async_remote_copy(
            src_ref=send.at[i], dst_ref=win.at[1, slot], send_sem=a_send.at[i], recv_sem=a_recv.at[slot],
            device_id=(i * CORES + 1 - c, (x + q // nz) % ngrp), device_id_type=MESH)

    def send_four(i):
        first = (q // 4 + i) % steps * 4
        for k in range(4):
            to_bin(first + k).start()

    def group_of(j):
        o = (j + 1 - q // 4 % 2) % ngrp
        return (x + o + ngrp - q // nz) % ngrp

    def forward(j, to):
        part = pl.ds(group_of(j) * nz, nz)
        return pltpu.make_async_remote_copy(
            src_ref=win.at[1, part], dst_ref=win.at[0 if to == 0 else 2, part],
            send_sem=f_send.at[to, j], recv_sem=f_recv.at[to, group_of(j)],
            device_id=((up if to == 0 else down) * CORES + c, x), device_id_type=MESH)

    def forward_group(j):
        def arrived(z, _):
            s = group_of(j) * nz + z
            pltpu.make_async_remote_copy(
                src_ref=send.at[0], dst_ref=win.at[1, s], send_sem=a_send.at[0], recv_sem=a_recv.at[s],
                device_id=(q * CORES + 1 - c, x), device_id_type=MESH).wait_recv()
            return 0

        lax.fori_loop(0, nz, arrived, 0)
        forward(j, 0).start()
        forward(j, 1).start()

    def order(i, _):
        for half in range(2):
            tile = (q // 4 + i) % steps * 2 + half
            acc = jnp.zeros((48, wide2), F32)
            for k in range(blocks // 2):
                cols = slice(k * wide2, (k + 1) * wide2)
                d = dcol[cols, :] - tile * wide2
                one = jnp.concatenate(
                    [jnp.where(d == lane2, 1.0, 0.0), jnp.where(d == lane2 + LANES, 1.0, 0.0)], axis=1).astype(BF16)
                acc = acc + dot(xp[:, cols], one)
            full = acc[:16] + acc[16:32] + acc[32:]
            send[2 * tile] = full[:ROWS, :LANES]
            send[2 * tile + 1] = full[:ROWS, LANES:]

        @pl.when(i == 1)
        def _():
            pl.semaphore_wait(barrier, nchip + 2 + members - 1)
            send_four(0)
            for o in range(1, members):
                pc, px = peer_of(me, o, ngrp)
                for ref, s_sem, r_sem in ((vols, v_send, v_recv), (lists, l_send, l_recv)):
                    pltpu.make_async_remote_copy(
                        src_ref=ref.at[me], dst_ref=ref.at[me], send_sem=s_sem.at[o], recv_sem=r_sem.at[o],
                        device_id=(q * CORES + pc, px), device_id_type=MESH).start()

        @pl.when(i >= 1)
        def _():
            send_four(i)

        @pl.when(i == 4)
        def _():
            forward_group(0)

        @pl.when(i == 6)
        def _():
            forward_group(1)

        return 0

    lax.fori_loop(0, steps, order, 0)
    for j in range(2, ngrp):
        forward_group(j)

    left = lax.broadcasted_iota(jnp.int32, (ROWS, LANES), 1) < span
    row8 = lax.broadcasted_iota(jnp.int32, (8, LANES), 0)

    def prepare(chip, g):
        for k in range(nz // 2):
            a = win[chip, g * nz + 2 * k]
            b = win[chip, g * nz + 2 * k + 1]
            pair = (jnp.where(left, a, pltpu.roll(b, span, 1)), jnp.where(left, pltpu.roll(a, span, 1), b))
            cols = slice(k * LANES, (k + 1) * LANES)
            for tt in range(CORES):
                n = (chip * CORES + tt) * ngrp + g
                upper = pair[tt][:8]
                lower = jnp.concatenate([pair[tt][8:], jnp.zeros((16 - ROWS, LANES), F32)], axis=0)
                m1, m2, _ = split3(jnp.where(row8 == 7, 1.0, upper))
                mt[n, :, cols] = jnp.concatenate([m1, m2], axis=0).astype(BF16)
                x2, yz2 = upper * upper, lower * lower
                norm = x2[7:8] + yz2[0:1] + yz2[1:2] + 0.01
                y = -2.0 * jnp.where(row8 == 7, upper, lower)
                y = jnp.where(row8 == 2, norm, jnp.where(row8 == 3, 1.0, y))
                y1, y2, y3 = split3(y)
                fs[n, :, cols] = jnp.concatenate([y1, y2, y3, y1, y2, y1], axis=0).astype(BF16)

    def prepare_own(g, _):
        prepare(1, g)
        return 0

    lax.fori_loop(0, ngrp, prepare_own, 0)

    def vol_copies(o):
        other = (me + members - o) % members
        pc, px = peer_of(me, o, ngrp)
        return [pltpu.make_async_remote_copy(
            src_ref=ref.at[me], dst_ref=ref.at[other], send_sem=s_sem.at[o], recv_sem=r_sem.at[o],
            device_id=(q * CORES + pc, px), device_id_type=MESH)
            for ref, s_sem, r_sem in ((vols, v_send, v_recv), (lists, l_send, l_recv))]

    for o in range(1, members):
        for copy in vol_copies(o):
            copy.wait_recv()

    def prepare_vol(j, _):
        v = vols[j]
        v2 = v * v
        norm = v2[0:1] + v2[1:2] + v2[2:3]
        ones = jnp.ones_like(norm)
        zero = jnp.zeros_like(norm)
        w1, w2, w3 = split3(jnp.concatenate([v[1:3], ones, norm, zero, zero, zero, v[0:1]], axis=0))
        fv[j] = jnp.concatenate([w1, w1, w1, w2, w2, w3], axis=0).astype(BF16)
        return 0

    lax.fori_loop(0, members, prepare_vol, 0)

    def arrived_near(j, _):
        for to in range(2):
            part = pl.ds(j * nz, nz)
            pltpu.make_async_remote_copy(
                src_ref=win.at[1, part], dst_ref=win.at[0 if to == 0 else 2, part],
                send_sem=f_send.at[to, 0], recv_sem=f_recv.at[to, j],
                device_id=((up if to == 0 else down) * CORES + c, x), device_id_type=MESH).wait_recv()
        prepare(0, j)
        prepare(2, j)
        return 0

    lax.fori_loop(0, ngrp, arrived_near, 0)

    def sent(i, _):
        to_bin(i).wait_send()
        return 0

    lax.fori_loop(0, nchip, sent, 0)
    for o in range(1, members):
        for copy in vol_copies(o):
            copy.wait_send()
    for j in range(ngrp):
        for to in range(2):
            forward(j, to).wait_send()


def exchange(nchip, ngrp, pos, mot, bins, vol, infl, cnt):
    members = CORES * ngrp
    nvol = vol.shape[1]
    width = pos.shape[1]
    nbin = 3 * CORES * ngrp
    nodes = nchip // ngrp * LANES // CORES
    dma = pltpu.SemaphoreType.DMA
    return pl.pallas_call(
        functools.partial(exchange_kernel, nchip, ngrp),
        out_shape=(
            jax.ShapeDtypeStruct((nbin, DEPTH, nodes), BF16),
            jax.ShapeDtypeStruct((nbin, 16, nodes), BF16),
            jax.ShapeDtypeStruct((members, DEPTH, nvol), BF16),
            jax.ShapeDtypeStruct((members, 1, LANES), jnp.int32),
        ),
        in_specs=[HBM, HBM, HBM, HBM, SMEM, SMEM],
        out_specs=(VMEM, VMEM, VMEM, VMEM),
        scratch_shapes=[
            pltpu.VMEM(pos.shape, F32),
            pltpu.VMEM(mot.shape, F32),
            pltpu.VMEM(bins.shape, jnp.int32),
            pltpu.VMEM((members, 3, nvol), F32),
            pltpu.VMEM((48, width), BF16),
            pltpu.VMEM((width, LANES), jnp.int32),
            pltpu.VMEM((nchip, ROWS, LANES), F32),
            pltpu.VMEM((3, nchip, ROWS, LANES), F32),
            dma((4,)),
            dma((nchip,)), dma((nchip,)),
            dma((2, ngrp)), dma((2, ngrp)),
            dma((members,)), dma((members,)),
            dma((members,)), dma((members,)),
        ],
        compiler_params=pltpu.CompilerParams(collective_id=0, has_side_effects=True, vmem_limit_bytes=40 << 20),
    )(pos, mot, bins, vol, infl, cnt)


def blend_kernel(ngrp, lmax, lists, fs, mt, fv, part, acc, block_of, bin_of):
    q, _, _ = place()
    members = fv.shape[0]
    base = (q - 1) * CORES * ngrp

    def block(j, filled):
        acc[j] = jnp.zeros(acc.shape[1:], F32)

        def entry(l, filled):
            block_of[filled] = j
            bin_of[filled] = lists[j, 0, l] - base
            return filled + 1

        return lax.fori_loop(0, lists[j, 0, lmax], entry, filled)

    total = lax.fori_loop(0, members, block, 0)

    def together(first, many):
        js = [block_of[first + k] for k in range(many)]
        ns = [bin_of[first + k] for k in range(many)]
        r2 = [dot(fs[n], fv[j], ((0,), (0,))) for j, n in zip(js, ns)]
        for j, n, d in zip(js, ns, r2):
            w = pltpu.reciprocal(d * d, approx=True)
            w1 = w.astype(BF16)
            w2 = (w - w1.astype(F32)).astype(BF16)
            m = mt[n]
            acc[j] += dot(m, w1) + dot(m, w2)

    def four(i, _):
        together(4 * i, 4)
        return 0

    def one(i, _):
        together(i, 1)
        return 0

    lax.fori_loop(0, total // 4, four, 0)
    lax.fori_loop(total // 4 * 4, total, one, 0)

    def close(j, _):
        part[j] = acc[j, :8] + acc[j, 8:]
        return 0

    lax.fori_loop(0, members, close, 0)


def blend(ngrp, lmax, lists, fs, mt, fv):
    members, _, nvol = fv.shape
    return pl.pallas_call(
        functools.partial(blend_kernel, ngrp, lmax),
        out_shape=jax.ShapeDtypeStruct((members, 8, nvol), F32),
        in_specs=[SMEM, VMEM, VMEM, VMEM],
        out_specs=VMEM,
        scratch_shapes=[
            pltpu.VMEM((members, 16, nvol), F32),
            pltpu.SMEM((members * lmax,), jnp.int32),
            pltpu.SMEM((members * lmax,), jnp.int32),
        ],
        compiler_params=pltpu.CompilerParams(vmem_limit_bytes=48 << 20),
    )(lists, fs, mt, fv)


def combine_kernel(ngrp, part, out, got, s_sem, r_sem):
    q, c, x = place()
    members = CORES * ngrp
    me = c * ngrp + x
    barrier = pltpu.get_barrier_semaphore()
    for o in range(1, members):
        pc, px = peer_of(me, o, ngrp)
        pl.semaphore_signal(barrier, inc=1, device_id=(q * CORES + pc, px), device_id_type=MESH)
    pl.semaphore_wait(barrier, members - 1)
    copies = []
    for o in range(1, members):
        pc, px = peer_of(me, o, ngrp)
        copy = pltpu.make_async_remote_copy(
            src_ref=part.at[(me + o) % members], dst_ref=got.at[o], send_sem=s_sem.at[o], recv_sem=r_sem.at[o],
            device_id=(q * CORES + pc, px), device_id_type=MESH)
        copy.start()
        copies.append(copy)
    total = part[me]
    for o in range(1, members):
        copies[o - 1].wait_recv()
        total = total + got[o]
    out[...] = total[:7] / total[7:8]
    for copy in copies:
        copy.wait_send()


def combine(ngrp, part):
    members, _, nvol = part.shape
    return pl.pallas_call(
        functools.partial(combine_kernel, ngrp),
        out_shape=jax.ShapeDtypeStruct((7, nvol), F32),
        in_specs=[VMEM],
        out_specs=VMEM,
        scratch_shapes=[
            pltpu.VMEM((members, 8, nvol), F32),
            pltpu.SemaphoreType.DMA((members,)),
            pltpu.SemaphoreType.DMA((members,)),
        ],
        compiler_params=pltpu.CompilerParams(collective_id=1, has_side_effects=True, vmem_limit_bytes=48 << 20),
    )(part)


def on_device(surf_pos, surf_motion, surf_bin, vol_pos, influence, list_count):
    nchip = lax.axis_size("slab") // CORES
    ngrp = lax.axis_size("grp")
    bins = surf_bin.reshape(-1, LANES)
    fs, mt, fv, lists = exchange(nchip, ngrp, surf_pos, surf_motion, bins, vol_pos, influence, list_count)
    part = blend(ngrp, influence.shape[1], lists, fs, mt, fv)
    return combine(ngrp, part)


def solution(mesh):
    return jax.shard_map(
        on_device,
        mesh=mesh,
        in_specs=(
            P(None, ("slab", "grp")),
            P(None, ("slab", "grp")),
            P(("slab", "grp")),
            P(None, ("slab", "grp")),
            P(("slab", "grp"), None),
            P(("slab", "grp")),
        ),
        out_specs=P(None, ("slab", "grp")),
        check_vma=False,
    )
```

```python
import functools

import jax
import jax.numpy as jnp
from jax import lax
from jax.experimental import pallas as pl
from jax.experimental.pallas import tpu as pltpu
from jax.sharding import PartitionSpec as P

F32, BF16 = jnp.float32, jnp.bfloat16
MESH = pl.DeviceIdType.MESH
VMEM = pl.BlockSpec(memory_space=pltpu.VMEM)
SMEM = pl.BlockSpec(memory_space=pltpu.SMEM)
HBM = pl.BlockSpec(memory_space=pltpu.HBM)
ROWS = 10
LANES = 128
CORES = 2
EARLY = 4
DEPTH = 48


def dot(a, b, dims=((1,), (0,))):
    return lax.dot_general(a, b, (dims, ((), ())), preferred_element_type=F32)


def split3(x):
    first = x.astype(BF16).astype(F32)
    rest = x - first
    second = rest.astype(BF16).astype(F32)
    return first, second, (rest - second).astype(BF16).astype(F32)


def place():
    slab = lax.axis_index("slab")
    return slab // CORES, slab % CORES, lax.axis_index("grp")


def peer_of(me, offset, ngrp):
    other = (me + offset) % (CORES * ngrp)
    return other // ngrp, other % ngrp


def exchange_kernel(nchip, ngrp, pos_in, mot_in, bins_in, vol_in, infl_in, cnt, fs, mt, fv, lists,
                    infl, pos, mot, bins, vols, xp, dcol, send, win,
                    in_sem, a_send, a_recv, f_send, f_recv, v_send, v_recv, l_send, l_recv):
    q, c, x = place()
    nz = nchip // ngrp
    blocks = bins.shape[0]
    nslab = nchip * CORES
    span = LANES // CORES
    members = CORES * ngrp
    me = c * ngrp + x
    up, down = (q + 1) % nchip, (q + nchip - 1) % nchip

    y, z, ny = q // nz, q % nz, nchip // nz

    def shift(i):
        j = i // nz
        return j + j // 2 * (1 - 2 * (j % 2))

    def chip_at(i, sign):
        kz, ky = i // ny, i % ny
        dz = nz // 2 + (kz + 1) // 2 * (1 - 2 * (kz % 2))
        dy = ny // 2 + (ky + 1) // 2 * (1 - 2 * (ky % 2))
        return (y + ny + sign * dy) % ny * nz + (z + nz + sign * dz) % nz

    def met(i, sign):
        return chip_at(i, sign) * CORES + c, (x + ngrp + sign * shift(i)) % ngrp

    loads = [pltpu.make_async_copy(bins_in, bins, in_sem.at[0]), pltpu.make_async_copy(mot_in, mot, in_sem.at[1]),
             pltpu.make_async_copy(pos_in, pos, in_sem.at[2]), pltpu.make_async_copy(vol_in, vols.at[me], in_sem.at[3]),
             pltpu.make_async_copy(infl_in, infl, in_sem.at[4])]
    for load in loads:
        load.start()

    barrier = pltpu.get_barrier_semaphore()

    def greet(device):
        pl.semaphore_signal(barrier, inc=1, device_id=device, device_id_type=MESH)

    def greet_source(i, carry):
        greet(met(i, -1))
        return carry

    lax.fori_loop(0, nchip, greet_source, 0)
    greet((up * CORES + c, x))
    greet((down * CORES + c, x))
    for o in range(1, members):
        pc, px = peer_of(me, o, ngrp)
        greet((q * CORES + pc, px))

    loads[0].wait()
    slab_of = bins[...] // ngrp
    sub = lax.broadcasted_iota(jnp.int32, (nslab, LANES), 0)
    tri_r = lax.broadcasted_iota(jnp.int32, (LANES, 2 * LANES), 0)
    tri_c = lax.broadcasted_iota(jnp.int32, (LANES, 2 * LANES), 1)
    tri = jnp.where((tri_r <= tri_c), 1.0, 0.0).astype(BF16)
    carry = jnp.zeros((nslab, LANES), F32)
    for k in range(blocks):
        trow = slab_of[k : k + 1, :]
        hit = trow == sub
        cum = dot(jnp.where(hit, 1.0, 0.0).astype(BF16), tri)
        rank = jnp.sum(jnp.where(hit, cum[:, :LANES] + carry, 0.0), axis=0, keepdims=True)
        carry = carry + cum[:, LANES:]
        dest = trow.astype(F32) * span + (rank - 1.0)
        wide = jnp.broadcast_to(dest, (LANES, LANES)).T
        dcol[k * LANES : (k + 1) * LANES, :] = wide.astype(jnp.int32)

    for load in loads[1:]:
        load.wait()
    lane = lax.broadcasted_iota(jnp.int32, (1, LANES), 1)
    row = jnp.where(lane == infl.shape[1], cnt[0], 0)
    for l in range(infl.shape[1]):
        row = jnp.where(lane == l, infl[0, l], row)
    lists[pl.ds(me, 1)] = row[None]

    whole = jnp.concatenate([mot[...], pos[...], jnp.zeros((16 - ROWS, mot.shape[1]), F32)], axis=0)
    xp[...] = jnp.concatenate(split3(whole), axis=0).astype(BF16)

    steps = nchip // 4
    lanes = lax.broadcasted_iota(jnp.int32, (1, LANES), 1)

    def to_bin(i):
        slot = x * nz + i % nz
        return pltpu.make_async_remote_copy(
            src_ref=send.at[i], dst_ref=win.at[1, slot], send_sem=a_send.at[i], recv_sem=a_recv.at[slot],
            device_id=met(i, 1), device_id_type=MESH)

    def send_one(i, _):
        to_bin(i).start()
        return 0

    def group_of(j):
        return (x + ngrp - shift(j * nz)) % ngrp

    def forward(j, to):
        part = pl.ds(group_of(j) * nz, nz)
        return pltpu.make_async_remote_copy(
            src_ref=win.at[1, part], dst_ref=win.at[0 if to == 0 else 2, part],
            send_sem=f_send.at[to, j], recv_sem=f_recv.at[to, j],
            device_id=((up if to == 0 else down) * CORES + c, x), device_id_type=MESH)

    def forward_group(j, _):
        def arrived(k, _):
            s = group_of(j) * nz + k
            pltpu.make_async_remote_copy(
                src_ref=send.at[0], dst_ref=win.at[1, s], send_sem=a_send.at[0], recv_sem=a_recv.at[s],
                device_id=met(0, 1), device_id_type=MESH).wait_recv()
            return 0

        lax.fori_loop(0, nz, arrived, 0)
        forward(j, 0).start()
        forward(j, 1).start()
        return 0

    def order(i, _):
        for half in range(2):
            r = 4 * i + 2 * half
            want = [jnp.broadcast_to(lanes + chip_at(r + k, 1) * LANES, (2 * LANES, LANES)) for k in range(2)]
            acc = jnp.zeros((48, 2 * LANES), F32)
            for k in range(blocks // 2):
                cols = slice(k * 2 * LANES, (k + 1) * 2 * LANES)
                d = dcol[cols, :]
                one = jnp.concatenate([jnp.where(d == w, 1.0, 0.0) for w in want], axis=1).astype(BF16)
                acc = acc + dot(xp[:, cols], one)
            full = acc[:16] + acc[16:32] + acc[32:]
            send[r] = full[:ROWS, :LANES]
            send[r + 1] = full[:ROWS, LANES:]

        @pl.when(i == EARLY)
        def _():
            pl.semaphore_wait(barrier, nchip + 2 + members - 1)
            lax.fori_loop(0, 4 * EARLY, send_one, 0)

        @pl.when(i >= EARLY)
        def _():
            lax.fori_loop(4 * i, 4 * i + 4, send_one, 0)

        @pl.when(i == EARLY)
        def _():
            for o in range(1, members):
                pc, px = peer_of(me, o, ngrp)
                for ref, s_sem, r_sem in ((vols, v_send, v_recv), (lists, l_send, l_recv)):
                    pltpu.make_async_remote_copy(
                        src_ref=ref.at[me], dst_ref=ref.at[me], send_sem=s_sem.at[o], recv_sem=r_sem.at[o],
                        device_id=(q * CORES + pc, px), device_id_type=MESH).start()

        return 0

    lax.fori_loop(0, steps, order, 0)
    lax.fori_loop(0, ngrp, forward_group, 0)

    left = lax.broadcasted_iota(jnp.int32, (ROWS, LANES), 1) < span
    row8 = lax.broadcasted_iota(jnp.int32, (8, LANES), 0)

    def prepare(chip, g):
        for k in range(nz // 2):
            a = win[chip, g * nz + 2 * k]
            b = win[chip, g * nz + 2 * k + 1]
            pair = (jnp.where(left, a, pltpu.roll(b, span, 1)), jnp.where(left, pltpu.roll(a, span, 1), b))
            cols = slice(k * LANES, (k + 1) * LANES)
            for tt in range(CORES):
                n = (chip * CORES + tt) * ngrp + g
                upper = pair[tt][:8]
                lower = jnp.concatenate([pair[tt][8:], jnp.zeros((16 - ROWS, LANES), F32)], axis=0)
                m1, m2, _ = split3(jnp.where(row8 == 7, 1.0, upper))
                mt[n, :, cols] = jnp.concatenate([m1, m2], axis=0).astype(BF16)
                x2, yz2 = upper * upper, lower * lower
                norm = x2[7:8] + yz2[0:1] + yz2[1:2] + 0.01
                y = -2.0 * jnp.where(row8 == 7, upper, lower)
                y = jnp.where(row8 == 2, norm, jnp.where(row8 == 3, 1.0, y))
                y1, y2, y3 = split3(y)
                fs[n, :, cols] = jnp.concatenate([y1, y2, y3, y1, y2, y1], axis=0).astype(BF16)

    def prepare_own(g, _):
        prepare(1, g)
        return 0

    lax.fori_loop(0, ngrp, prepare_own, 0)

    def vol_copies(o):
        other = (me + members - o) % members
        pc, px = peer_of(me, o, ngrp)
        return [pltpu.make_async_remote_copy(
            src_ref=ref.at[me], dst_ref=ref.at[other], send_sem=s_sem.at[o], recv_sem=r_sem.at[o],
            device_id=(q * CORES + pc, px), device_id_type=MESH)
            for ref, s_sem, r_sem in ((vols, v_send, v_recv), (lists, l_send, l_recv))]

    for o in range(1, members):
        for copy in vol_copies(o):
            copy.wait_recv()

    def prepare_vol(j, _):
        v = vols[j]
        v2 = v * v
        norm = v2[0:1] + v2[1:2] + v2[2:3]
        ones = jnp.ones_like(norm)
        zero = jnp.zeros_like(norm)
        w1, w2, w3 = split3(jnp.concatenate([v[1:3], ones, norm, zero, zero, zero, v[0:1]], axis=0))
        fv[j] = jnp.concatenate([w1, w1, w1, w2, w2, w3], axis=0).astype(BF16)
        return 0

    lax.fori_loop(0, members, prepare_vol, 0)

    def arrived_near(j, _):
        for to in range(2):
            forward(j, to).wait_recv()
        prepare(0, group_of(j))
        prepare(2, group_of(j))
        return 0

    lax.fori_loop(0, ngrp, arrived_near, 0)

    def sent(i, _):
        to_bin(i).wait_send()
        return 0

    lax.fori_loop(0, nchip, sent, 0)
    for o in range(1, members):
        for copy in vol_copies(o):
            copy.wait_send()
    for j in range(ngrp):
        for to in range(2):
            forward(j, to).wait_send()


def exchange(nchip, ngrp, pos, mot, bins, vol, infl, cnt):
    members = CORES * ngrp
    nvol = vol.shape[1]
    width = pos.shape[1]
    nbin = 3 * CORES * ngrp
    nodes = nchip // ngrp * LANES // CORES
    dma = pltpu.SemaphoreType.DMA
    return pl.pallas_call(
        functools.partial(exchange_kernel, nchip, ngrp),
        out_shape=(
            jax.ShapeDtypeStruct((nbin, DEPTH, nodes), BF16),
            jax.ShapeDtypeStruct((nbin, 16, nodes), BF16),
            jax.ShapeDtypeStruct((members, DEPTH, nvol), BF16),
            jax.ShapeDtypeStruct((members, 1, LANES), jnp.int32),
        ),
        in_specs=[HBM] * 5 + [SMEM],
        out_specs=(VMEM, VMEM, VMEM, VMEM),
        scratch_shapes=[
            pltpu.SMEM(infl.shape, jnp.int32),
            pltpu.VMEM(pos.shape, F32),
            pltpu.VMEM(mot.shape, F32),
            pltpu.VMEM(bins.shape, jnp.int32),
            pltpu.VMEM((members, 3, nvol), F32),
            pltpu.VMEM((48, width), BF16),
            pltpu.VMEM((width, LANES), jnp.int32),
            pltpu.VMEM((nchip, ROWS, LANES), F32),
            pltpu.VMEM((3, nchip, ROWS, LANES), F32),
            dma((5,)),
            dma((nchip,)), dma((nchip,)),
            dma((2, ngrp)), dma((2, ngrp)),
            dma((members,)), dma((members,)),
            dma((members,)), dma((members,)),
        ],
        compiler_params=pltpu.CompilerParams(collective_id=0, has_side_effects=True, vmem_limit_bytes=40 << 20),
    )(pos, mot, bins, vol, infl, cnt)


def blend_kernel(ngrp, lmax, lists, fs, mt, fv, part, acc, block_of, bin_of):
    q, _, _ = place()
    members = fv.shape[0]
    base = (q - 1) * CORES * ngrp

    def block(j, filled):
        acc[j] = jnp.zeros(acc.shape[1:], F32)

        def entry(l, filled):
            block_of[filled] = j
            bin_of[filled] = lists[j, 0, l] - base
            return filled + 1

        return lax.fori_loop(0, lists[j, 0, lmax], entry, filled)

    total = lax.fori_loop(0, members, block, 0)

    def together(first, many):
        js = [block_of[first + k] for k in range(many)]
        ns = [bin_of[first + k] for k in range(many)]
        r2 = [dot(fs[n], fv[j], ((0,), (0,))) for j, n in zip(js, ns)]
        for j, n, d in zip(js, ns, r2):
            w = pltpu.reciprocal(d * d, approx=True)
            w1 = w.astype(BF16)
            w2 = (w - w1.astype(F32)).astype(BF16)
            m = mt[n]
            acc[j] += dot(m, w1) + dot(m, w2)

    def four(i, _):
        together(4 * i, 4)
        return 0

    def one(i, _):
        together(i, 1)
        return 0

    lax.fori_loop(0, total // 4, four, 0)
    lax.fori_loop(total // 4 * 4, total, one, 0)

    def close(j, _):
        part[j] = acc[j, :8] + acc[j, 8:]
        return 0

    lax.fori_loop(0, members, close, 0)


def blend(ngrp, lmax, lists, fs, mt, fv):
    members, _, nvol = fv.shape
    return pl.pallas_call(
        functools.partial(blend_kernel, ngrp, lmax),
        out_shape=jax.ShapeDtypeStruct((members, 8, nvol), F32),
        in_specs=[SMEM, VMEM, VMEM, VMEM],
        out_specs=VMEM,
        scratch_shapes=[
            pltpu.VMEM((members, 16, nvol), F32),
            pltpu.SMEM((members * lmax,), jnp.int32),
            pltpu.SMEM((members * lmax,), jnp.int32),
        ],
        compiler_params=pltpu.CompilerParams(vmem_limit_bytes=48 << 20),
    )(lists, fs, mt, fv)


def combine_kernel(ngrp, part, out, got, s_sem, r_sem):
    q, c, x = place()
    members = CORES * ngrp
    me = c * ngrp + x
    barrier = pltpu.get_barrier_semaphore()
    for o in range(1, members):
        pc, px = peer_of(me, o, ngrp)
        pl.semaphore_signal(barrier, inc=1, device_id=(q * CORES + pc, px), device_id_type=MESH)
    pl.semaphore_wait(barrier, members - 1)
    copies = []
    for o in range(1, members):
        pc, px = peer_of(me, o, ngrp)
        copy = pltpu.make_async_remote_copy(
            src_ref=part.at[(me + o) % members], dst_ref=got.at[o], send_sem=s_sem.at[o], recv_sem=r_sem.at[o],
            device_id=(q * CORES + pc, px), device_id_type=MESH)
        copy.start()
        copies.append(copy)
    total = part[me]
    for o in range(1, members):
        copies[o - 1].wait_recv()
        total = total + got[o]
    out[...] = total[:7] / total[7:8]
    for copy in copies:
        copy.wait_send()


def combine(ngrp, part):
    members, _, nvol = part.shape
    return pl.pallas_call(
        functools.partial(combine_kernel, ngrp),
        out_shape=jax.ShapeDtypeStruct((7, nvol), F32),
        in_specs=[VMEM],
        out_specs=VMEM,
        scratch_shapes=[
            pltpu.VMEM((members, 8, nvol), F32),
            pltpu.SemaphoreType.DMA((members,)),
            pltpu.SemaphoreType.DMA((members,)),
        ],
        compiler_params=pltpu.CompilerParams(collective_id=1, has_side_effects=True, vmem_limit_bytes=48 << 20),
    )(part)


def on_device(surf_pos, surf_motion, surf_bin, vol_pos, influence, list_count):
    nchip = lax.axis_size("slab") // CORES
    ngrp = lax.axis_size("grp")
    bins = surf_bin.reshape(-1, LANES)
    surf_pos, surf_motion, bins, vol_pos, influence = (
        pltpu.with_memory_space_constraint(a, pltpu.HBM) for a in (surf_pos, surf_motion, bins, vol_pos, influence))
    fs, mt, fv, lists = exchange(nchip, ngrp, surf_pos, surf_motion, bins, vol_pos, influence, list_count)
    part = blend(ngrp, influence.shape[1], lists, fs, mt, fv)
    return combine(ngrp, part)


def solution(mesh):
    return jax.shard_map(
        on_device,
        mesh=mesh,
        in_specs=(
            P(None, ("slab", "grp")),
            P(None, ("slab", "grp")),
            P(("slab", "grp")),
            P(None, ("slab", "grp")),
            P(("slab", "grp"), None),
            P(("slab", "grp")),
        ),
        out_specs=P(None, ("slab", "grp")),
        check_vma=False,
    )
```

```python
import functools

import jax
import jax.numpy as jnp
from jax import lax
from jax.experimental import pallas as pl
from jax.experimental.pallas import tpu as pltpu
from jax.sharding import PartitionSpec as P

F32, BF16 = jnp.float32, jnp.bfloat16
MESH = pl.DeviceIdType.MESH
VMEM = pl.BlockSpec(memory_space=pltpu.VMEM)
SMEM = pl.BlockSpec(memory_space=pltpu.SMEM)
HBM = pl.BlockSpec(memory_space=pltpu.HBM)
ROWS = 10
LANES = 128
CORES = 2
DEPTH = 48


def dot(a, b, dims=((1,), (0,))):
    return lax.dot_general(a, b, (dims, ((), ())), preferred_element_type=F32)


def split3(x):
    first = x.astype(BF16).astype(F32)
    rest = x - first
    second = rest.astype(BF16).astype(F32)
    return first, second, (rest - second).astype(BF16).astype(F32)


def place():
    slab = lax.axis_index("slab")
    return slab // CORES, slab % CORES, lax.axis_index("grp")


def peer_of(me, offset, ngrp):
    other = (me + offset) % (CORES * ngrp)
    return other // ngrp, other % ngrp


def exchange_kernel(nchip, ngrp, pos_in, mot_in, bins_in, vol_in, infl_in, cnt, fs, mt, fv, lists,
                    infl, pos, mot, bins, vols, xp, one, acc, send, win,
                    in_sem, a_send, a_recv, f_send, f_recv, v_send, v_recv, l_send, l_recv):
    q, c, x = place()
    nz = nchip // ngrp
    blocks = bins.shape[0]
    nslab = nchip * CORES
    span = LANES // CORES
    members = CORES * ngrp
    me = c * ngrp + x
    up, down = (q + 1) % nchip, (q + nchip - 1) % nchip

    y, z, ny = q // nz, q % nz, nchip // nz

    def shift(i):
        j = i // nz
        return j + j // 2 * (1 - 2 * (j % 2))

    def chip_at(i, sign):
        kz, ky = i // ny, i % ny
        dz = nz // 2 + (kz + 1) // 2 * (1 - 2 * (kz % 2))
        dy = ny // 2 + (ky + 1) // 2 * (1 - 2 * (ky % 2))
        return (y + ny + sign * dy) % ny * nz + (z + nz + sign * dz) % nz

    def met(i, sign):
        return chip_at(i, sign) * CORES + c, (x + ngrp + sign * shift(i)) % ngrp

    loads = [pltpu.make_async_copy(bins_in, bins, in_sem.at[0]), pltpu.make_async_copy(mot_in, mot, in_sem.at[1]),
             pltpu.make_async_copy(pos_in, pos, in_sem.at[2]), pltpu.make_async_copy(vol_in, vols.at[me], in_sem.at[3]),
             pltpu.make_async_copy(infl_in, infl, in_sem.at[4])]
    for load in loads:
        load.start()

    barrier = pltpu.get_barrier_semaphore()

    def greet(device):
        pl.semaphore_signal(barrier, inc=1, device_id=device, device_id_type=MESH)

    def greet_source(i, carry):
        greet(met(i, -1))
        return carry

    lax.fori_loop(0, nchip, greet_source, 0)
    greet((up * CORES + c, x))
    greet((down * CORES + c, x))
    for o in range(1, members):
        pc, px = peer_of(me, o, ngrp)
        greet((q * CORES + pc, px))

    loads[0].wait()
    slab_of = bins[...] // ngrp
    sub = lax.broadcasted_iota(jnp.int32, (nslab, LANES), 0)
    tri_r = lax.broadcasted_iota(jnp.int32, (LANES, 2 * LANES), 0)
    tri_c = lax.broadcasted_iota(jnp.int32, (LANES, 2 * LANES), 1)
    tri = jnp.where((tri_r <= tri_c), 1.0, 0.0).astype(BF16)
    carry = jnp.zeros((nslab, LANES), F32)
    fold = 2 * LANES // span
    column = lax.broadcasted_iota(jnp.int32, (LANES, LANES), 1).astype(F32)
    for k in range(blocks):
        trow = slab_of[k : k + 1, :]
        hit = trow == sub
        cum = dot(jnp.where(hit, 1.0, 0.0).astype(BF16), tri)
        rank = jnp.sum(jnp.where(hit, cum[:, :LANES] + carry, 0.0), axis=0, keepdims=True)
        carry = carry + cum[:, LANES:]
        dest = (trow % fold * span).astype(F32) + (rank - 1.0)
        wide = jnp.broadcast_to(dest, (LANES, LANES)).T
        one[k * LANES : (k + 1) * LANES, :] = jnp.concatenate(
            [jnp.where(wide == column + h * LANES, 1.0, 0.0) for h in range(2)], axis=1).astype(BF16)

    for load in loads[1:]:
        load.wait()
    lane = lax.broadcasted_iota(jnp.int32, (1, LANES), 1)
    row = jnp.where(lane == infl.shape[1], cnt[0], 0)
    for l in range(infl.shape[1]):
        row = jnp.where(lane == l, infl[0, l], row)
    lists[pl.ds(me, 1)] = row[None]

    whole = jnp.concatenate([mot[...], pos[...], jnp.zeros((16 - ROWS, mot.shape[1]), F32)], axis=0)
    xp[...] = jnp.concatenate(split3(whole), axis=0)

    def to_bin(i):
        slot = x * nz + i % nz
        return pltpu.make_async_remote_copy(
            src_ref=send.at[chip_at(i, 1)], dst_ref=win.at[1, slot], send_sem=a_send.at[i], recv_sem=a_recv.at[slot],
            device_id=met(i, 1), device_id_type=MESH)

    def send_one(i, _):
        to_bin(i).start()
        return 0

    def group_of(j):
        return (x + ngrp - shift(j * nz)) % ngrp

    def forward(j, to):
        part = pl.ds(group_of(j) * nz, nz)
        return pltpu.make_async_remote_copy(
            src_ref=win.at[1, part], dst_ref=win.at[0 if to == 0 else 2, part],
            send_sem=f_send.at[to, j], recv_sem=f_recv.at[to, j],
            device_id=((up if to == 0 else down) * CORES + c, x), device_id_type=MESH)

    def forward_group(j, _):
        def arrived(k, _):
            s = group_of(j) * nz + k
            pltpu.make_async_remote_copy(
                src_ref=send.at[0], dst_ref=win.at[1, s], send_sem=a_send.at[0], recv_sem=a_recv.at[s],
                device_id=met(0, 1), device_id_type=MESH).wait_recv()
            return 0

        lax.fori_loop(0, nz, arrived, 0)
        forward(j, 0).start()
        forward(j, 1).start()
        return 0

    tiles = slab_of // fold
    ntile = nslab // fold
    rows = 4
    for k in range(blocks // rows):
        cols = slice(k * rows * LANES, (k + 1) * rows * LANES)
        mine = jnp.concatenate([tiles[k * rows + r : k * rows + r + 1, :] for r in range(rows)], axis=1)
        piece = xp[:, cols]
        kept = jnp.concatenate([jnp.where(mine == p, piece, 0.0) for p in range(ntile)], axis=0).astype(BF16)
        product = dot(kept, one[cols, :])
        acc[...] = product if k == 0 else acc[...] + product
    for p in range(ntile):
        full = acc[48 * p : 48 * p + 16] + acc[48 * p + 16 : 48 * p + 32] + acc[48 * p + 32 : 48 * p + 48]
        send[2 * p] = full[:ROWS, :LANES]
        send[2 * p + 1] = full[:ROWS, LANES:]

    pl.semaphore_wait(barrier, nchip + 2 + members - 1)
    lax.fori_loop(0, nchip, send_one, 0)
    for o in range(1, members):
        pc, px = peer_of(me, o, ngrp)
        for ref, s_sem, r_sem in ((vols, v_send, v_recv), (lists, l_send, l_recv)):
            pltpu.make_async_remote_copy(
                src_ref=ref.at[me], dst_ref=ref.at[me], send_sem=s_sem.at[o], recv_sem=r_sem.at[o],
                device_id=(q * CORES + pc, px), device_id_type=MESH).start()
    lax.fori_loop(0, ngrp, forward_group, 0)

    left = lax.broadcasted_iota(jnp.int32, (ROWS, LANES), 1) < span
    row8 = lax.broadcasted_iota(jnp.int32, (8, LANES), 0)

    def prepare(chip, g):
        for k in range(nz // 2):
            a = win[chip, g * nz + 2 * k]
            b = win[chip, g * nz + 2 * k + 1]
            pair = (jnp.where(left, a, pltpu.roll(b, span, 1)), jnp.where(left, pltpu.roll(a, span, 1), b))
            cols = slice(k * LANES, (k + 1) * LANES)
            for tt in range(CORES):
                n = (chip * CORES + tt) * ngrp + g
                upper = pair[tt][:8]
                lower = jnp.concatenate([pair[tt][8:], jnp.zeros((16 - ROWS, LANES), F32)], axis=0)
                m1, m2, _ = split3(jnp.where(row8 == 7, 1.0, upper))
                mt[n, :, cols] = jnp.concatenate([m1, m2], axis=0).astype(BF16)
                x2, yz2 = upper * upper, lower * lower
                norm = x2[7:8] + yz2[0:1] + yz2[1:2] + 0.01
                y = -2.0 * jnp.where(row8 == 7, upper, lower)
                y = jnp.where(row8 == 2, norm, jnp.where(row8 == 3, 1.0, y))
                y1, y2, y3 = split3(y)
                fs[n, :, cols] = jnp.concatenate([y1, y2, y3, y1, y2, y1], axis=0).astype(BF16)

    def prepare_own(g, _):
        prepare(1, g)
        return 0

    lax.fori_loop(0, ngrp, prepare_own, 0)

    def vol_copies(o):
        other = (me + members - o) % members
        pc, px = peer_of(me, o, ngrp)
        return [pltpu.make_async_remote_copy(
            src_ref=ref.at[me], dst_ref=ref.at[other], send_sem=s_sem.at[o], recv_sem=r_sem.at[o],
            device_id=(q * CORES + pc, px), device_id_type=MESH)
            for ref, s_sem, r_sem in ((vols, v_send, v_recv), (lists, l_send, l_recv))]

    for o in range(1, members):
        for copy in vol_copies(o):
            copy.wait_recv()

    def prepare_vol(j, _):
        v = vols[j]
        v2 = v * v
        norm = v2[0:1] + v2[1:2] + v2[2:3]
        ones = jnp.ones_like(norm)
        zero = jnp.zeros_like(norm)
        w1, w2, w3 = split3(jnp.concatenate([v[1:3], ones, norm, zero, zero, zero, v[0:1]], axis=0))
        fv[j] = jnp.concatenate([w1, w1, w1, w2, w2, w3], axis=0).astype(BF16)
        return 0

    lax.fori_loop(0, members, prepare_vol, 0)

    def arrived_near(j, _):
        for to in range(2):
            forward(j, to).wait_recv()
        prepare(0, group_of(j))
        prepare(2, group_of(j))
        return 0

    lax.fori_loop(0, ngrp, arrived_near, 0)

    def sent(i, _):
        to_bin(i).wait_send()
        return 0

    lax.fori_loop(0, nchip, sent, 0)
    for o in range(1, members):
        for copy in vol_copies(o):
            copy.wait_send()
    for j in range(ngrp):
        for to in range(2):
            forward(j, to).wait_send()


def exchange(nchip, ngrp, pos, mot, bins, vol, infl, cnt):
    members = CORES * ngrp
    nvol = vol.shape[1]
    width = pos.shape[1]
    nbin = 3 * CORES * ngrp
    nodes = nchip // ngrp * LANES // CORES
    dma = pltpu.SemaphoreType.DMA
    return pl.pallas_call(
        functools.partial(exchange_kernel, nchip, ngrp),
        out_shape=(
            jax.ShapeDtypeStruct((nbin, DEPTH, nodes), BF16),
            jax.ShapeDtypeStruct((nbin, 16, nodes), BF16),
            jax.ShapeDtypeStruct((members, DEPTH, nvol), BF16),
            jax.ShapeDtypeStruct((members, 1, LANES), jnp.int32),
        ),
        in_specs=[HBM] * 5 + [SMEM],
        out_specs=(VMEM, VMEM, VMEM, VMEM),
        scratch_shapes=[
            pltpu.SMEM(infl.shape, jnp.int32),
            pltpu.VMEM(pos.shape, F32),
            pltpu.VMEM(mot.shape, F32),
            pltpu.VMEM(bins.shape, jnp.int32),
            pltpu.VMEM((members, 3, nvol), F32),
            pltpu.VMEM((48, width), F32),
            pltpu.VMEM((width, 2 * LANES), BF16),
            pltpu.VMEM((nchip // 2 * 48, 2 * LANES), F32),
            pltpu.VMEM((nchip, ROWS, LANES), F32),
            pltpu.VMEM((3, nchip, ROWS, LANES), F32),
            dma((5,)),
            dma((nchip,)), dma((nchip,)),
            dma((2, ngrp)), dma((2, ngrp)),
            dma((members,)), dma((members,)),
            dma((members,)), dma((members,)),
        ],
        compiler_params=pltpu.CompilerParams(collective_id=0, has_side_effects=True, vmem_limit_bytes=40 << 20),
    )(pos, mot, bins, vol, infl, cnt)


def blend_kernel(ngrp, lmax, lists, fs, mt, fv, part, acc, block_of, bin_of):
    q, _, _ = place()
    members = fv.shape[0]
    base = (q - 1) * CORES * ngrp

    def block(j, filled):
        acc[j] = jnp.zeros(acc.shape[1:], F32)

        def entry(l, filled):
            block_of[filled] = j
            bin_of[filled] = lists[j, 0, l] - base
            return filled + 1

        return lax.fori_loop(0, lists[j, 0, lmax], entry, filled)

    total = lax.fori_loop(0, members, block, 0)

    def together(first, many):
        js = [block_of[first + k] for k in range(many)]
        ns = [bin_of[first + k] for k in range(many)]
        r2 = [dot(fs[n], fv[j], ((0,), (0,))) for j, n in zip(js, ns)]
        for j, n, d in zip(js, ns, r2):
            w = pltpu.reciprocal(d * d, approx=True)
            w1 = w.astype(BF16)
            w2 = (w - w1.astype(F32)).astype(BF16)
            m = mt[n]
            acc[j] += dot(m, w1) + dot(m, w2)

    def four(i, _):
        together(4 * i, 4)
        return 0

    def one(i, _):
        together(i, 1)
        return 0

    lax.fori_loop(0, total // 4, four, 0)
    lax.fori_loop(total // 4 * 4, total, one, 0)

    def close(j, _):
        part[j] = acc[j, :8] + acc[j, 8:]
        return 0

    lax.fori_loop(0, members, close, 0)


def blend(ngrp, lmax, lists, fs, mt, fv):
    members, _, nvol = fv.shape
    return pl.pallas_call(
        functools.partial(blend_kernel, ngrp, lmax),
        out_shape=jax.ShapeDtypeStruct((members, 8, nvol), F32),
        in_specs=[SMEM, VMEM, VMEM, VMEM],
        out_specs=VMEM,
        scratch_shapes=[
            pltpu.VMEM((members, 16, nvol), F32),
            pltpu.SMEM((members * lmax,), jnp.int32),
            pltpu.SMEM((members * lmax,), jnp.int32),
        ],
        compiler_params=pltpu.CompilerParams(vmem_limit_bytes=48 << 20),
    )(lists, fs, mt, fv)


def combine_kernel(ngrp, part, out, across, along, sums, c_send, c_recv, x_send, x_recv):
    q, c, x = place()
    barrier = pltpu.get_barrier_semaphore()
    there = (q * CORES + 1 - c, x)
    pl.semaphore_signal(barrier, inc=1, device_id=there, device_id_type=MESH)
    for o in range(1, ngrp):
        pl.semaphore_signal(barrier, inc=1, device_id=(q * CORES + c, (x + o) % ngrp), device_id_type=MESH)
    pl.semaphore_wait(barrier, ngrp)

    crossing = []
    for o in (2, 1, 3, 0):
        to = (x + o) % ngrp
        copy = pltpu.make_async_remote_copy(
            src_ref=part.at[(1 - c) * ngrp + to], dst_ref=across.at[to], send_sem=c_send.at[to], recv_sem=c_recv.at[to],
            device_id=there, device_id_type=MESH)
        copy.start()
        crossing.append((o, to, copy))
    moving = []
    for o, to, copy in crossing[:-1]:
        copy.wait_recv()
        sums[o] = part[c * ngrp + to] + across[to]
        step = pltpu.make_async_remote_copy(
            src_ref=sums.at[o], dst_ref=along.at[o], send_sem=x_send.at[o], recv_sem=x_recv.at[o],
            device_id=(q * CORES + c, to), device_id_type=MESH)
        step.start()
        moving.append((o, step))
    crossing[-1][2].wait_recv()
    total = part[c * ngrp + x] + across[x]
    for o, step in moving:
        step.wait_recv()
        total = total + along[o]
    out[...] = total[:7] / total[7:8]
    for _, _, copy in crossing:
        copy.wait_send()
    for _, step in moving:
        step.wait_send()


def combine(ngrp, part):
    nvol = part.shape[2]
    return pl.pallas_call(
        functools.partial(combine_kernel, ngrp),
        out_shape=jax.ShapeDtypeStruct((7, nvol), F32),
        in_specs=[VMEM],
        out_specs=VMEM,
        scratch_shapes=[pltpu.VMEM((ngrp, 8, nvol), F32)] * 3 + [pltpu.SemaphoreType.DMA((ngrp,))] * 4,
        compiler_params=pltpu.CompilerParams(collective_id=1, has_side_effects=True, vmem_limit_bytes=48 << 20),
    )(part)


def on_device(surf_pos, surf_motion, surf_bin, vol_pos, influence, list_count):
    nchip = lax.axis_size("slab") // CORES
    ngrp = lax.axis_size("grp")
    bins = surf_bin.reshape(-1, LANES)
    surf_pos, surf_motion, bins, vol_pos, influence = (
        pltpu.with_memory_space_constraint(a, pltpu.HBM) for a in (surf_pos, surf_motion, bins, vol_pos, influence))
    fs, mt, fv, lists = exchange(nchip, ngrp, surf_pos, surf_motion, bins, vol_pos, influence, list_count)
    part = blend(ngrp, influence.shape[1], lists, fs, mt, fv)
    return combine(ngrp, part)


def solution(mesh):
    return jax.shard_map(
        on_device,
        mesh=mesh,
        in_specs=(
            P(None, ("slab", "grp")),
            P(None, ("slab", "grp")),
            P(("slab", "grp")),
            P(None, ("slab", "grp")),
            P(("slab", "grp"), None),
            P(("slab", "grp")),
        ),
        out_specs=P(None, ("slab", "grp")),
        check_vma=False,
    )
```

```python
import functools

import jax
import jax.numpy as jnp
from jax import lax
from jax.experimental import pallas as pl
from jax.experimental.pallas import tpu as pltpu
from jax.sharding import PartitionSpec as P

F32, BF16 = jnp.float32, jnp.bfloat16
MESH = pl.DeviceIdType.MESH
VMEM = pl.BlockSpec(memory_space=pltpu.VMEM)
SMEM = pl.BlockSpec(memory_space=pltpu.SMEM)
HBM = pl.BlockSpec(memory_space=pltpu.HBM)
ROWS = 10
LANES = 128
CORES = 2
LATE = 2
DEPTH = 48


def dot(a, b, dims=((1,), (0,))):
    return lax.dot_general(a, b, (dims, ((), ())), preferred_element_type=F32)


def split3(x):
    first = x.astype(BF16).astype(F32)
    rest = x - first
    second = rest.astype(BF16).astype(F32)
    return first, second, (rest - second).astype(BF16).astype(F32)


def place():
    slab = lax.axis_index("slab")
    return slab // CORES, slab % CORES, lax.axis_index("grp")


def peer_of(me, offset, ngrp):
    other = (me + offset) % (CORES * ngrp)
    return other // ngrp, other % ngrp


def exchange_kernel(nchip, ngrp, pos_in, mot_in, bins_in, vol_in, infl_in, cnt, fs, mt, fv, lists,
                    infl, pos, mot, bins, vols, xp, one, acc, send, win,
                    in_sem, a_send, a_recv, f_send, f_recv, v_send, v_recv, l_send, l_recv):
    q, c, x = place()
    nz = nchip // ngrp
    blocks = bins.shape[0]
    nslab = nchip * CORES
    span = LANES // CORES
    members = CORES * ngrp
    me = c * ngrp + x
    up, down = (q + 1) % nchip, (q + nchip - 1) % nchip

    y, z, ny = q // nz, q % nz, nchip // nz

    def shift(i):
        j = i // nz
        return j + j // 2 * (1 - 2 * (j % 2))

    def chip_at(i, sign):
        kz, ky = i // ny, i % ny
        dz = nz // 2 + (kz + 1) // 2 * (1 - 2 * (kz % 2))
        dy = ny // 2 + (ky + 1) // 2 * (1 - 2 * (ky % 2))
        return (y + ny + sign * dy) % ny * nz + (z + nz + sign * dz) % nz

    def met(i, sign):
        return chip_at(i, sign) * CORES + c, (x + ngrp + sign * shift(i)) % ngrp

    loads = [pltpu.make_async_copy(bins_in, bins, in_sem.at[0]), pltpu.make_async_copy(mot_in, mot, in_sem.at[1]),
             pltpu.make_async_copy(pos_in, pos, in_sem.at[2]), pltpu.make_async_copy(vol_in, vols.at[me], in_sem.at[3]),
             pltpu.make_async_copy(infl_in, infl, in_sem.at[4])]
    for load in loads:
        load.start()

    barrier = pltpu.get_barrier_semaphore()

    def greet(device):
        pl.semaphore_signal(barrier, inc=1, device_id=device, device_id_type=MESH)

    def greet_source(i, carry):
        greet(met(i, -1))
        return carry

    lax.fori_loop(0, nchip, greet_source, 0)
    greet((up * CORES + c, x))
    greet((down * CORES + c, x))
    for o in range(1, members):
        pc, px = peer_of(me, o, ngrp)
        greet((q * CORES + pc, px))

    loads[0].wait()
    slab_of = bins[...] // ngrp
    sub = lax.broadcasted_iota(jnp.int32, (nslab, LANES), 0)
    tri_r = lax.broadcasted_iota(jnp.int32, (LANES, 2 * LANES), 0)
    tri_c = lax.broadcasted_iota(jnp.int32, (LANES, 2 * LANES), 1)
    tri = jnp.where((tri_r <= tri_c), 1.0, 0.0).astype(BF16)
    carry = jnp.zeros((nslab, LANES), F32)
    fold = 2 * LANES // span
    column = lax.broadcasted_iota(jnp.int32, (LANES, LANES), 1).astype(F32)
    for k in range(blocks):
        trow = slab_of[k : k + 1, :]
        hit = trow == sub
        cum = dot(jnp.where(hit, 1.0, 0.0).astype(BF16), tri)
        rank = jnp.sum(jnp.where(hit, cum[:, :LANES] + carry, 0.0), axis=0, keepdims=True)
        carry = carry + cum[:, LANES:]
        dest = (trow % fold * span).astype(F32) + (rank - 1.0)
        wide = jnp.broadcast_to(dest, (LANES, LANES)).T
        one[k * LANES : (k + 1) * LANES, :] = jnp.concatenate(
            [jnp.where(wide == column + h * LANES, 1.0, 0.0) for h in range(2)], axis=1).astype(BF16)

    for load in loads[1:]:
        load.wait()
    lane = lax.broadcasted_iota(jnp.int32, (1, LANES), 1)
    row = jnp.where(lane == infl.shape[1], cnt[0], 0)
    for l in range(infl.shape[1]):
        row = jnp.where(lane == l, infl[0, l], row)
    lists[pl.ds(me, 1)] = row[None]

    whole = jnp.concatenate([mot[...], pos[...], jnp.zeros((16 - ROWS, mot.shape[1]), F32)], axis=0)
    xp[...] = jnp.concatenate(split3(whole), axis=0)

    def to_bin(i):
        slot = x * nz + i % nz
        return pltpu.make_async_remote_copy(
            src_ref=send.at[chip_at(i, 1)], dst_ref=win.at[1, slot], send_sem=a_send.at[i], recv_sem=a_recv.at[slot],
            device_id=met(i, 1), device_id_type=MESH)

    def send_one(i, _):
        to_bin(i).start()
        return 0

    def group_of(j):
        return (x + ngrp - shift(j * nz)) % ngrp

    def forward(j, to):
        part = pl.ds(group_of(j) * nz, nz)
        return pltpu.make_async_remote_copy(
            src_ref=win.at[1, part], dst_ref=win.at[0 if to == 0 else 2, part],
            send_sem=f_send.at[to, j], recv_sem=f_recv.at[to, j],
            device_id=((up if to == 0 else down) * CORES + c, x), device_id_type=MESH)

    def forward_group(j, _):
        def arrived(k, _):
            s = group_of(j) * nz + k
            pltpu.make_async_remote_copy(
                src_ref=send.at[0], dst_ref=win.at[1, s], send_sem=a_send.at[0], recv_sem=a_recv.at[s],
                device_id=met(0, 1), device_id_type=MESH).wait_recv()
            return 0

        lax.fori_loop(0, nz, arrived, 0)
        forward(j, 0).start()
        forward(j, 1).start()
        return 0

    tiles = slab_of // fold
    ntile = nslab // fold
    rows = 4
    for k in range(blocks // rows):
        cols = slice(k * rows * LANES, (k + 1) * rows * LANES)
        mine = jnp.concatenate([tiles[k * rows + r : k * rows + r + 1, :] for r in range(rows)], axis=1)
        piece = xp[:, cols]
        kept = jnp.concatenate([jnp.where(mine == p, piece, 0.0) for p in range(ntile)], axis=0).astype(BF16)
        product = dot(kept, one[cols, :])
        acc[...] = product if k == 0 else acc[...] + product
    for p in range(ntile):
        full = acc[48 * p : 48 * p + 16] + acc[48 * p + 16 : 48 * p + 32] + acc[48 * p + 32 : 48 * p + 48]
        send[2 * p] = full[:ROWS, :LANES]
        send[2 * p + 1] = full[:ROWS, LANES:]

    pl.semaphore_wait(barrier, nchip + 2 + members - 1)
    lax.fori_loop(0, nchip, send_one, 0)
    for o in range(1, members):
        pc, px = peer_of(me, o, ngrp)
        for ref, s_sem, r_sem in ((vols, v_send, v_recv), (lists, l_send, l_recv)):
            pltpu.make_async_remote_copy(
                src_ref=ref.at[me], dst_ref=ref.at[me], send_sem=s_sem.at[o], recv_sem=r_sem.at[o],
                device_id=(q * CORES + pc, px), device_id_type=MESH).start()
    lax.fori_loop(0, ngrp, forward_group, 0)

    left = lax.broadcasted_iota(jnp.int32, (ROWS, LANES), 1) < span
    row8 = lax.broadcasted_iota(jnp.int32, (8, LANES), 0)

    def prepare(chip, g):
        for k in range(nz // 2):
            a = win[chip, g * nz + 2 * k]
            b = win[chip, g * nz + 2 * k + 1]
            pair = (jnp.where(left, a, pltpu.roll(b, span, 1)), jnp.where(left, pltpu.roll(a, span, 1), b))
            cols = slice(k * LANES, (k + 1) * LANES)
            for tt in range(CORES):
                n = (chip * CORES + tt) * ngrp + g
                upper = pair[tt][:8]
                lower = jnp.concatenate([pair[tt][8:], jnp.zeros((16 - ROWS, LANES), F32)], axis=0)
                m1, m2, _ = split3(jnp.where(row8 == 7, 1.0, upper))
                mt[n, :, cols] = jnp.concatenate([m1, m2], axis=0).astype(BF16)
                x2, yz2 = upper * upper, lower * lower
                norm = x2[7:8] + yz2[0:1] + yz2[1:2] + 0.01
                y = -2.0 * jnp.where(row8 == 7, upper, lower)
                y = jnp.where(row8 == 2, norm, jnp.where(row8 == 3, 1.0, y))
                y1, y2, y3 = split3(y)
                fs[n, :, cols] = jnp.concatenate([y1, y2, y3, y1, y2, y1], axis=0).astype(BF16)

    def prepare_own(g, _):
        prepare(1, g)
        return 0

    lax.fori_loop(0, ngrp, prepare_own, 0)

    def vol_copies(o):
        other = (me + members - o) % members
        pc, px = peer_of(me, o, ngrp)
        return [pltpu.make_async_remote_copy(
            src_ref=ref.at[me], dst_ref=ref.at[other], send_sem=s_sem.at[o], recv_sem=r_sem.at[o],
            device_id=(q * CORES + pc, px), device_id_type=MESH)
            for ref, s_sem, r_sem in ((vols, v_send, v_recv), (lists, l_send, l_recv))]

    for o in range(1, members):
        for copy in vol_copies(o):
            copy.wait_recv()

    def prepare_vol(j, _):
        v = vols[j]
        v2 = v * v
        norm = v2[0:1] + v2[1:2] + v2[2:3]
        ones = jnp.ones_like(norm)
        zero = jnp.zeros_like(norm)
        w1, w2, w3 = split3(jnp.concatenate([v[1:3], ones, norm, zero, zero, zero, v[0:1]], axis=0))
        fv[j] = jnp.concatenate([w1, w1, w1, w2, w2, w3], axis=0).astype(BF16)
        return 0

    lax.fori_loop(0, members, prepare_vol, 0)

    def arrived_near(j, _):
        for to in range(2):
            forward(j, to).wait_recv()
        prepare(0, group_of(j))
        prepare(2, group_of(j))
        return 0

    lax.fori_loop(0, ngrp, arrived_near, 0)

    def sent(i, _):
        to_bin(i).wait_send()
        return 0

    lax.fori_loop(0, nchip, sent, 0)
    for o in range(1, members):
        for copy in vol_copies(o):
            copy.wait_send()
    for j in range(ngrp):
        for to in range(2):
            forward(j, to).wait_send()


def exchange(nchip, ngrp, pos, mot, bins, vol, infl, cnt):
    members = CORES * ngrp
    nvol = vol.shape[1]
    width = pos.shape[1]
    nbin = 3 * CORES * ngrp
    nodes = nchip // ngrp * LANES // CORES
    dma = pltpu.SemaphoreType.DMA
    return pl.pallas_call(
        functools.partial(exchange_kernel, nchip, ngrp),
        out_shape=(
            jax.ShapeDtypeStruct((nbin, DEPTH, nodes), BF16),
            jax.ShapeDtypeStruct((nbin, 16, nodes), BF16),
            jax.ShapeDtypeStruct((members, DEPTH, nvol), BF16),
            jax.ShapeDtypeStruct((members, 1, LANES), jnp.int32),
        ),
        in_specs=[HBM] * 5 + [SMEM],
        out_specs=(VMEM, VMEM, VMEM, VMEM),
        scratch_shapes=[
            pltpu.SMEM(infl.shape, jnp.int32),
            pltpu.VMEM(pos.shape, F32),
            pltpu.VMEM(mot.shape, F32),
            pltpu.VMEM(bins.shape, jnp.int32),
            pltpu.VMEM((members, 3, nvol), F32),
            pltpu.VMEM((48, width), F32),
            pltpu.VMEM((width, 2 * LANES), BF16),
            pltpu.VMEM((nchip // 2 * 48, 2 * LANES), F32),
            pltpu.VMEM((nchip, ROWS, LANES), F32),
            pltpu.VMEM((3, nchip, ROWS, LANES), F32),
            dma((5,)),
            dma((nchip,)), dma((nchip,)),
            dma((2, ngrp)), dma((2, ngrp)),
            dma((members,)), dma((members,)),
            dma((members,)), dma((members,)),
        ],
        compiler_params=pltpu.CompilerParams(collective_id=0, has_side_effects=True, vmem_limit_bytes=40 << 20),
    )(pos, mot, bins, vol, infl, cnt)


def blended(fs, mt, fv, ns, js):
    r2 = [dot(fs[n], fv[j], ((0,), (0,))) for n, j in zip(ns, js)]
    sums = []
    for n, d in zip(ns, r2):
        w = pltpu.reciprocal(d * d, approx=True)
        w1 = w.astype(BF16)
        w2 = (w - w1.astype(F32)).astype(BF16)
        m = mt[n]
        sums.append(dot(m, w1) + dot(m, w2))
    return sums


def blend_kernel(ngrp, lmax, lists, fs, mt, fv, part, acc, block_of, bin_of):
    q, _, x = place()
    members = fv.shape[0]
    base = (q - 1) * CORES * ngrp

    def block(j, filled):
        acc[j] = jnp.zeros(acc.shape[1:], F32)

        def entry(l, filled):
            block_of[filled] = j
            bin_of[filled] = lists[j, 0, l] - base
            return filled + 1

        return lax.fori_loop(jnp.where(j % ngrp == x, LATE, 0), lists[j, 0, lmax], entry, filled)

    total = lax.fori_loop(0, members, block, 0)

    def together(first, many):
        js = [block_of[first + k] for k in range(many)]
        ns = [bin_of[first + k] for k in range(many)]
        for j, more in zip(js, blended(fs, mt, fv, ns, js)):
            acc[j] += more

    def four(i, _):
        together(4 * i, 4)
        return 0

    def one(i, _):
        together(i, 1)
        return 0

    lax.fori_loop(0, total // 4, four, 0)
    lax.fori_loop(total // 4 * 4, total, one, 0)

    def close(j, _):
        part[j] = acc[j, :8] + acc[j, 8:]
        return 0

    lax.fori_loop(0, members, close, 0)


def blend(ngrp, lmax, lists, fs, mt, fv):
    members, _, nvol = fv.shape
    return pl.pallas_call(
        functools.partial(blend_kernel, ngrp, lmax),
        out_shape=jax.ShapeDtypeStruct((members, 8, nvol), F32),
        in_specs=[SMEM, VMEM, VMEM, VMEM],
        out_specs=VMEM,
        scratch_shapes=[
            pltpu.VMEM((members, 16, nvol), F32),
            pltpu.SMEM((members * lmax,), jnp.int32),
            pltpu.SMEM((members * lmax,), jnp.int32),
        ],
        compiler_params=pltpu.CompilerParams(vmem_limit_bytes=48 << 20),
    )(lists, fs, mt, fv)


def combine_kernel(ngrp, lists, fs, mt, fv, part, out, across, along, sums, c_send, c_recv, x_send, x_recv):
    q, c, x = place()
    base = (q - 1) * CORES * ngrp

    def late(j):
        ns = [jnp.clip(lists[j, 0, l] - base, 0, fs.shape[0] - 1) for l in range(LATE)]
        more = sum(blended(fs, mt, fv, ns, [j] * LATE))
        return part[j] + (more[:8] + more[8:])

    barrier = pltpu.get_barrier_semaphore()
    there = (q * CORES + 1 - c, x)
    pl.semaphore_signal(barrier, inc=1, device_id=there, device_id_type=MESH)
    for o in range(1, ngrp):
        pl.semaphore_signal(barrier, inc=1, device_id=(q * CORES + c, (x + o) % ngrp), device_id_type=MESH)
    pl.semaphore_wait(barrier, ngrp)

    def cross(to, src):
        copy = pltpu.make_async_remote_copy(
            src_ref=src, dst_ref=across.at[to], send_sem=c_send.at[to], recv_sem=c_recv.at[to],
            device_id=there, device_id_type=MESH)
        copy.start()
        return copy

    others = [(o, (x + o) % ngrp) for o in (2, 1, 3)]
    crossing = [cross(to, part.at[(1 - c) * ngrp + to]) for _, to in others]
    moving = []
    for (o, to), copy in zip(others, crossing):
        copy.wait_recv()
        sums[o] = part[c * ngrp + to] + across[to]
        step = pltpu.make_async_remote_copy(
            src_ref=sums.at[o], dst_ref=along.at[o], send_sem=x_send.at[o], recv_sem=x_recv.at[o],
            device_id=(q * CORES + c, to), device_id_type=MESH)
        step.start()
        moving.append((o, step))

    sums[0] = late((1 - c) * ngrp + x)
    last = cross(x, sums.at[0])
    total = late(c * ngrp + x)
    for o, step in moving:
        step.wait_recv()
        total = total + along[o]
    last.wait_recv()
    total = total + across[x]
    out[...] = total[:7] / total[7:8]
    for copy in crossing + [last]:
        copy.wait_send()
    for _, step in moving:
        step.wait_send()


def combine(ngrp, lists, fs, mt, fv, part):
    nvol = part.shape[2]
    return pl.pallas_call(
        functools.partial(combine_kernel, ngrp),
        out_shape=jax.ShapeDtypeStruct((7, nvol), F32),
        in_specs=[SMEM] + [VMEM] * 4,
        out_specs=VMEM,
        scratch_shapes=[pltpu.VMEM((ngrp, 8, nvol), F32)] * 3 + [pltpu.SemaphoreType.DMA((ngrp,))] * 4,
        compiler_params=pltpu.CompilerParams(collective_id=1, has_side_effects=True, vmem_limit_bytes=48 << 20),
    )(lists, fs, mt, fv, part)


def on_device(surf_pos, surf_motion, surf_bin, vol_pos, influence, list_count):
    nchip = lax.axis_size("slab") // CORES
    ngrp = lax.axis_size("grp")
    bins = surf_bin.reshape(-1, LANES)
    surf_pos, surf_motion, bins, vol_pos, influence = (
        pltpu.with_memory_space_constraint(a, pltpu.HBM) for a in (surf_pos, surf_motion, bins, vol_pos, influence))
    fs, mt, fv, lists = exchange(nchip, ngrp, surf_pos, surf_motion, bins, vol_pos, influence, list_count)
    part = blend(ngrp, influence.shape[1], lists, fs, mt, fv)
    return combine(ngrp, lists, fs, mt, fv, part)


def solution(mesh):
    return jax.shard_map(
        on_device,
        mesh=mesh,
        in_specs=(
            P(None, ("slab", "grp")),
            P(None, ("slab", "grp")),
            P(("slab", "grp")),
            P(None, ("slab", "grp")),
            P(("slab", "grp"), None),
            P(("slab", "grp")),
        ),
        out_specs=P(None, ("slab", "grp")),
        check_vma=False,
    )
```

```python
import functools

import jax
import jax.numpy as jnp
from jax import lax
from jax.experimental import pallas as pl
from jax.experimental.pallas import tpu as pltpu
from jax.sharding import PartitionSpec as P

F32, BF16 = jnp.float32, jnp.bfloat16
MESH = pl.DeviceIdType.MESH
VMEM = pl.BlockSpec(memory_space=pltpu.VMEM)
SMEM = pl.BlockSpec(memory_space=pltpu.SMEM)
HBM = pl.BlockSpec(memory_space=pltpu.HBM)
ROWS = 10
LANES = 128
CORES = 2
LATE = 2
DEPTH = 48


def dot(a, b, dims=((1,), (0,))):
    return lax.dot_general(a, b, (dims, ((), ())), preferred_element_type=F32)


def split3(x):
    first = x.astype(BF16).astype(F32)
    rest = x - first
    second = rest.astype(BF16).astype(F32)
    return first, second, (rest - second).astype(BF16).astype(F32)


def place():
    slab = lax.axis_index("slab")
    return slab // CORES, slab % CORES, lax.axis_index("grp")


def peer_of(me, offset, ngrp):
    other = (me + offset) % (CORES * ngrp)
    return other // ngrp, other % ngrp


def exchange_kernel(nchip, ngrp, pos_in, mot_in, bins_in, vol_in, infl_in, cnt, fs, mt, fv, lists,
                    infl, pos, mot, bins, vols, xp, one, acc, send, win,
                    in_sem, a_send, a_recv, f_send, f_recv, v_send, v_recv, l_send, l_recv):
    q, c, x = place()
    nz = nchip // ngrp
    blocks = bins.shape[0]
    nslab = nchip * CORES
    span = LANES // CORES
    members = CORES * ngrp
    me = c * ngrp + x
    up, down = (q + 1) % nchip, (q + nchip - 1) % nchip

    y, z, ny = q // nz, q % nz, nchip // nz

    def shift(i):
        j = i // nz
        return j + j // 2 * (1 - 2 * (j % 2))

    def chip_at(i, sign):
        kz, ky = i // ny, i % ny
        dz = nz // 2 + (kz + 1) // 2 * (1 - 2 * (kz % 2))
        dy = ny // 2 + (ky + 1) // 2 * (1 - 2 * (ky % 2))
        return lax.rem(y + ny + sign * dy, ny) * nz + lax.rem(z + nz + sign * dz, nz)

    def met(i, sign):
        return chip_at(i, sign) * CORES + c, lax.rem(x + ngrp + sign * shift(i), ngrp)

    loads = [pltpu.make_async_copy(bins_in, bins, in_sem.at[0]), pltpu.make_async_copy(mot_in, mot, in_sem.at[1]),
             pltpu.make_async_copy(pos_in, pos, in_sem.at[2]), pltpu.make_async_copy(vol_in, vols.at[me], in_sem.at[3]),
             pltpu.make_async_copy(infl_in, infl, in_sem.at[4])]
    for load in loads:
        load.start()

    barrier = pltpu.get_barrier_semaphore()

    def greet(device):
        pl.semaphore_signal(barrier, inc=1, device_id=device, device_id_type=MESH)

    for i in range(nchip):
        greet(met(i, -1))
    greet((up * CORES + c, x))
    greet((down * CORES + c, x))
    for o in range(1, members):
        pc, px = peer_of(me, o, ngrp)
        greet((q * CORES + pc, px))

    loads[0].wait()
    slab_of = bins[...] // ngrp
    sub = lax.broadcasted_iota(jnp.int32, (nslab, LANES), 0)
    tri_r = lax.broadcasted_iota(jnp.int32, (LANES, 2 * LANES), 0)
    tri_c = lax.broadcasted_iota(jnp.int32, (LANES, 2 * LANES), 1)
    tri = jnp.where((tri_r <= tri_c), 1.0, 0.0).astype(BF16)
    carry = jnp.zeros((nslab, LANES), F32)
    fold = 2 * LANES // span
    column = lax.broadcasted_iota(jnp.int32, (LANES, LANES), 1).astype(F32)
    for k in range(blocks):
        trow = slab_of[k : k + 1, :]
        hit = trow == sub
        cum = dot(jnp.where(hit, 1.0, 0.0).astype(BF16), tri)
        rank = jnp.sum(jnp.where(hit, cum[:, :LANES] + carry, 0.0), axis=0, keepdims=True)
        carry = carry + cum[:, LANES:]
        dest = (trow % fold * span).astype(F32) + (rank - 1.0)
        wide = jnp.broadcast_to(dest, (LANES, LANES)).T
        one[k * LANES : (k + 1) * LANES, :] = jnp.concatenate(
            [jnp.where(wide == column + h * LANES, 1.0, 0.0) for h in range(2)], axis=1).astype(BF16)

    for load in loads[1:]:
        load.wait()
    lane = lax.broadcasted_iota(jnp.int32, (1, LANES), 1)
    row = jnp.where(lane == infl.shape[1], cnt[0], 0)
    for l in range(infl.shape[1]):
        row = jnp.where(lane == l, infl[0, l], row)
    lists[pl.ds(me, 1)] = row[None]

    whole = jnp.concatenate([mot[...], pos[...], jnp.zeros((16 - ROWS, mot.shape[1]), F32)], axis=0)
    xp[...] = jnp.concatenate(split3(whole), axis=0)

    def to_bin(i):
        slot = x * nz + i % nz
        return pltpu.make_async_remote_copy(
            src_ref=send.at[chip_at(i, 1)], dst_ref=win.at[1, slot], send_sem=a_send.at[i], recv_sem=a_recv.at[slot],
            device_id=met(i, 1), device_id_type=MESH)

    def group_of(j):
        return (x + ngrp - shift(j * nz)) % ngrp

    def forward(j, to):
        part = pl.ds(group_of(j) * nz, nz)
        return pltpu.make_async_remote_copy(
            src_ref=win.at[1, part], dst_ref=win.at[0 if to == 0 else 2, part],
            send_sem=f_send.at[to, j], recv_sem=f_recv.at[to, j],
            device_id=((up if to == 0 else down) * CORES + c, x), device_id_type=MESH)

    def forward_group(j, _):
        def arrived(k, _):
            s = group_of(j) * nz + k
            pltpu.make_async_remote_copy(
                src_ref=send.at[0], dst_ref=win.at[1, s], send_sem=a_send.at[0], recv_sem=a_recv.at[s],
                device_id=met(0, 1), device_id_type=MESH).wait_recv()
            return 0

        lax.fori_loop(0, nz, arrived, 0)
        forward(j, 0).start()
        forward(j, 1).start()
        return 0

    tiles = slab_of // fold
    ntile = nslab // fold
    rows = 4
    for k in range(blocks // rows):
        cols = slice(k * rows * LANES, (k + 1) * rows * LANES)
        mine = jnp.concatenate([tiles[k * rows + r : k * rows + r + 1, :] for r in range(rows)], axis=1)
        piece = xp[:, cols]
        kept = jnp.concatenate([jnp.where(mine == p, piece, 0.0) for p in range(ntile)], axis=0).astype(BF16)
        product = dot(kept, one[cols, :])
        acc[...] = product if k == 0 else acc[...] + product
    for p in range(ntile):
        full = acc[48 * p : 48 * p + 16] + acc[48 * p + 16 : 48 * p + 32] + acc[48 * p + 32 : 48 * p + 48]
        send[2 * p] = full[:ROWS, :LANES]
        send[2 * p + 1] = full[:ROWS, LANES:]

    pl.semaphore_wait(barrier, nchip + 2 + members - 1)
    for i in range(nchip):
        to_bin(i).start()
    for o in range(1, members):
        pc, px = peer_of(me, o, ngrp)
        for ref, s_sem, r_sem in ((vols, v_send, v_recv), (lists, l_send, l_recv)):
            pltpu.make_async_remote_copy(
                src_ref=ref.at[me], dst_ref=ref.at[me], send_sem=s_sem.at[o], recv_sem=r_sem.at[o],
                device_id=(q * CORES + pc, px), device_id_type=MESH).start()
    lax.fori_loop(0, ngrp, forward_group, 0)

    left = lax.broadcasted_iota(jnp.int32, (ROWS, LANES), 1) < span
    row8 = lax.broadcasted_iota(jnp.int32, (8, LANES), 0)

    def prepare(chip, g):
        for k in range(nz // 2):
            a = win[chip, g * nz + 2 * k]
            b = win[chip, g * nz + 2 * k + 1]
            pair = (jnp.where(left, a, pltpu.roll(b, span, 1)), jnp.where(left, pltpu.roll(a, span, 1), b))
            cols = slice(k * LANES, (k + 1) * LANES)
            for tt in range(CORES):
                n = (chip * CORES + tt) * ngrp + g
                upper = pair[tt][:8]
                lower = jnp.concatenate([pair[tt][8:], jnp.zeros((16 - ROWS, LANES), F32)], axis=0)
                m1, m2, _ = split3(jnp.where(row8 == 7, 1.0, upper))
                mt[n, :, cols] = jnp.concatenate([m1, m2], axis=0).astype(BF16)
                x2, yz2 = upper * upper, lower * lower
                norm = x2[7:8] + yz2[0:1] + yz2[1:2] + 0.01
                y = -2.0 * jnp.where(row8 == 7, upper, lower)
                y = jnp.where(row8 == 2, norm, jnp.where(row8 == 3, 1.0, y))
                y1, y2, y3 = split3(y)
                fs[n, :, cols] = jnp.concatenate([y1, y2, y3, y1, y2, y1], axis=0).astype(BF16)

    def prepare_own(g, _):
        prepare(1, g)
        return 0

    lax.fori_loop(0, ngrp, prepare_own, 0)

    def vol_copies(o):
        other = (me + members - o) % members
        pc, px = peer_of(me, o, ngrp)
        return [pltpu.make_async_remote_copy(
            src_ref=ref.at[me], dst_ref=ref.at[other], send_sem=s_sem.at[o], recv_sem=r_sem.at[o],
            device_id=(q * CORES + pc, px), device_id_type=MESH)
            for ref, s_sem, r_sem in ((vols, v_send, v_recv), (lists, l_send, l_recv))]

    for o in range(1, members):
        for copy in vol_copies(o):
            copy.wait_recv()

    def prepare_vol(j, _):
        v = vols[j]
        v2 = v * v
        norm = v2[0:1] + v2[1:2] + v2[2:3]
        ones = jnp.ones_like(norm)
        zero = jnp.zeros_like(norm)
        w1, w2, w3 = split3(jnp.concatenate([v[1:3], ones, norm, zero, zero, zero, v[0:1]], axis=0))
        fv[j] = jnp.concatenate([w1, w1, w1, w2, w2, w3], axis=0).astype(BF16)
        return 0

    lax.fori_loop(0, members, prepare_vol, 0)

    def arrived_near(j, _):
        for to in range(2):
            forward(j, to).wait_recv()
        prepare(0, group_of(j))
        prepare(2, group_of(j))
        return 0

    lax.fori_loop(0, ngrp, arrived_near, 0)

    def sent(i, _):
        to_bin(i).wait_send()
        return 0

    lax.fori_loop(0, nchip, sent, 0)
    for o in range(1, members):
        for copy in vol_copies(o):
            copy.wait_send()
    for j in range(ngrp):
        for to in range(2):
            forward(j, to).wait_send()


def exchange(nchip, ngrp, pos, mot, bins, vol, infl, cnt):
    members = CORES * ngrp
    nvol = vol.shape[1]
    width = pos.shape[1]
    nbin = 3 * CORES * ngrp
    nodes = nchip // ngrp * LANES // CORES
    dma = pltpu.SemaphoreType.DMA
    return pl.pallas_call(
        functools.partial(exchange_kernel, nchip, ngrp),
        out_shape=(
            jax.ShapeDtypeStruct((nbin, DEPTH, nodes), BF16),
            jax.ShapeDtypeStruct((nbin, 16, nodes), BF16),
            jax.ShapeDtypeStruct((members, DEPTH, nvol), BF16),
            jax.ShapeDtypeStruct((members, 1, LANES), jnp.int32),
        ),
        in_specs=[HBM] * 5 + [SMEM],
        out_specs=(VMEM, VMEM, VMEM, VMEM),
        scratch_shapes=[
            pltpu.SMEM(infl.shape, jnp.int32),
            pltpu.VMEM(pos.shape, F32),
            pltpu.VMEM(mot.shape, F32),
            pltpu.VMEM(bins.shape, jnp.int32),
            pltpu.VMEM((members, 3, nvol), F32),
            pltpu.VMEM((48, width), F32),
            pltpu.VMEM((width, 2 * LANES), BF16),
            pltpu.VMEM((nchip // 2 * 48, 2 * LANES), F32),
            pltpu.VMEM((nchip, ROWS, LANES), F32),
            pltpu.VMEM((3, nchip, ROWS, LANES), F32),
            dma((5,)),
            dma((nchip,)), dma((nchip,)),
            dma((2, ngrp)), dma((2, ngrp)),
            dma((members,)), dma((members,)),
            dma((members,)), dma((members,)),
        ],
        compiler_params=pltpu.CompilerParams(collective_id=0, has_side_effects=True, vmem_limit_bytes=40 << 20),
    )(pos, mot, bins, vol, infl, cnt)


def blended(fs, mt, fv, ns, js):
    r2 = [dot(fs[n], fv[j], ((0,), (0,))) for n, j in zip(ns, js)]
    sums = []
    for n, d in zip(ns, r2):
        w = pltpu.reciprocal(d * d, approx=True)
        w1 = w.astype(BF16)
        w2 = (w - w1.astype(F32)).astype(BF16)
        m = mt[n]
        sums.append(dot(m, w1) + dot(m, w2))
    return sums


def blend_kernel(ngrp, lmax, lists, fs, mt, fv, part, acc, block_of, bin_of):
    q, _, x = place()
    members = fv.shape[0]
    base = (q - 1) * CORES * ngrp

    def block(j, filled):
        acc[j] = jnp.zeros(acc.shape[1:], F32)

        def entry(l, filled):
            block_of[filled] = j
            bin_of[filled] = lists[j, 0, l] - base
            return filled + 1

        return lax.fori_loop(jnp.where(j % ngrp == x, LATE, 0), lists[j, 0, lmax], entry, filled)

    total = lax.fori_loop(0, members, block, 0)

    def together(first, many):
        js = [block_of[first + k] for k in range(many)]
        ns = [bin_of[first + k] for k in range(many)]
        for j, more in zip(js, blended(fs, mt, fv, ns, js)):
            acc[j] += more

    def four(i, _):
        together(4 * i, 4)
        return 0

    def one(i, _):
        together(i, 1)
        return 0

    lax.fori_loop(0, total // 4, four, 0)
    lax.fori_loop(total // 4 * 4, total, one, 0)

    def close(j, _):
        part[j] = acc[j, :8] + acc[j, 8:]
        return 0

    lax.fori_loop(0, members, close, 0)


def blend(ngrp, lmax, lists, fs, mt, fv):
    members, _, nvol = fv.shape
    return pl.pallas_call(
        functools.partial(blend_kernel, ngrp, lmax),
        out_shape=jax.ShapeDtypeStruct((members, 8, nvol), F32),
        in_specs=[SMEM, VMEM, VMEM, VMEM],
        out_specs=VMEM,
        scratch_shapes=[
            pltpu.VMEM((members, 16, nvol), F32),
            pltpu.SMEM((members * lmax,), jnp.int32),
            pltpu.SMEM((members * lmax,), jnp.int32),
        ],
        compiler_params=pltpu.CompilerParams(vmem_limit_bytes=48 << 20),
    )(lists, fs, mt, fv)


def combine_kernel(ngrp, lists, fs, mt, fv, part, out, across, along, sums, c_send, c_recv, x_send, x_recv):
    q, c, x = place()
    base = (q - 1) * CORES * ngrp

    def late(j):
        ns = [jnp.clip(lists[j, 0, l] - base, 0, fs.shape[0] - 1) for l in range(LATE)]
        more = sum(blended(fs, mt, fv, ns, [j] * LATE))
        return part[j] + (more[:8] + more[8:])

    barrier = pltpu.get_barrier_semaphore()
    there = (q * CORES + 1 - c, x)
    pl.semaphore_signal(barrier, inc=1, device_id=there, device_id_type=MESH)
    for o in range(1, ngrp):
        pl.semaphore_signal(barrier, inc=1, device_id=(q * CORES + c, (x + o) % ngrp), device_id_type=MESH)
    pl.semaphore_wait(barrier, ngrp)

    def cross(to, src):
        copy = pltpu.make_async_remote_copy(
            src_ref=src, dst_ref=across.at[to], send_sem=c_send.at[to], recv_sem=c_recv.at[to],
            device_id=there, device_id_type=MESH)
        copy.start()
        return copy

    others = [(o, (x + o) % ngrp) for o in (2, 1, 3)]
    crossing = [cross(to, part.at[(1 - c) * ngrp + to]) for _, to in others]
    moving = []
    for (o, to), copy in zip(others, crossing):
        copy.wait_recv()
        sums[o] = part[c * ngrp + to] + across[to]
        step = pltpu.make_async_remote_copy(
            src_ref=sums.at[o], dst_ref=along.at[o], send_sem=x_send.at[o], recv_sem=x_recv.at[o],
            device_id=(q * CORES + c, to), device_id_type=MESH)
        step.start()
        moving.append((o, step))

    sums[0] = late((1 - c) * ngrp + x)
    last = cross(x, sums.at[0])
    total = late(c * ngrp + x)
    for o, step in moving:
        step.wait_recv()
        total = total + along[o]
    last.wait_recv()
    total = total + across[x]
    out[...] = total[:7] / total[7:8]
    for copy in crossing + [last]:
        copy.wait_send()
    for _, step in moving:
        step.wait_send()


def combine(ngrp, lists, fs, mt, fv, part):
    nvol = part.shape[2]
    return pl.pallas_call(
        functools.partial(combine_kernel, ngrp),
        out_shape=jax.ShapeDtypeStruct((7, nvol), F32),
        in_specs=[SMEM] + [VMEM] * 4,
        out_specs=VMEM,
        scratch_shapes=[pltpu.VMEM((ngrp, 8, nvol), F32)] * 3 + [pltpu.SemaphoreType.DMA((ngrp,))] * 4,
        compiler_params=pltpu.CompilerParams(collective_id=1, has_side_effects=True, vmem_limit_bytes=48 << 20),
    )(lists, fs, mt, fv, part)


def on_device(surf_pos, surf_motion, surf_bin, vol_pos, influence, list_count):
    nchip = lax.axis_size("slab") // CORES
    ngrp = lax.axis_size("grp")
    bins = surf_bin.reshape(-1, LANES)
    surf_pos, surf_motion, bins, vol_pos, influence = (
        pltpu.with_memory_space_constraint(a, pltpu.HBM) for a in (surf_pos, surf_motion, bins, vol_pos, influence))
    fs, mt, fv, lists = exchange(nchip, ngrp, surf_pos, surf_motion, bins, vol_pos, influence, list_count)
    part = blend(ngrp, influence.shape[1], lists, fs, mt, fv)
    return combine(ngrp, lists, fs, mt, fv, part)


def solution(mesh):
    return jax.shard_map(
        on_device,
        mesh=mesh,
        in_specs=(
            P(None, ("slab", "grp")),
            P(None, ("slab", "grp")),
            P(("slab", "grp")),
            P(None, ("slab", "grp")),
            P(("slab", "grp"), None),
            P(("slab", "grp")),
        ),
        out_specs=P(None, ("slab", "grp")),
        check_vma=False,
    )
```

```python
import functools

import jax
import jax.numpy as jnp
from jax import lax
from jax.experimental import pallas as pl
from jax.experimental.pallas import tpu as pltpu
from jax.sharding import PartitionSpec as P

F32, BF16 = jnp.float32, jnp.bfloat16
MESH = pl.DeviceIdType.MESH
VMEM = pl.BlockSpec(memory_space=pltpu.VMEM)
SMEM = pl.BlockSpec(memory_space=pltpu.SMEM)
HBM = pl.BlockSpec(memory_space=pltpu.HBM)
ROWS = 10
LANES = 128
CORES = 2
LATE = 2
DEPTH = 48


def dot(a, b, dims=((1,), (0,))):
    return lax.dot_general(a, b, (dims, ((), ())), preferred_element_type=F32)


def split3(x):
    first = x.astype(BF16).astype(F32)
    rest = x - first
    second = rest.astype(BF16).astype(F32)
    return first, second, (rest - second).astype(BF16).astype(F32)


def place():
    slab = lax.axis_index("slab")
    return slab // CORES, slab % CORES, lax.axis_index("grp")


def peer_of(me, offset, ngrp):
    other = (me + offset) % (CORES * ngrp)
    return other // ngrp, other % ngrp


def exchange_kernel(nchip, ngrp, pos_in, mot_in, bins_in, vol_in, infl_in, cnt, fs, mt, fv, lists,
                    infl, pos, mot, bins, vols, xp, one, acc, send, win,
                    in_sem, a_send, a_recv, f_send, f_recv, v_send, v_recv, l_send, l_recv):
    q, c, x = place()
    nz = nchip // ngrp
    blocks = bins.shape[0]
    nslab = nchip * CORES
    span = LANES // CORES
    members = CORES * ngrp
    me = c * ngrp + x
    up, down = (q + 1) % nchip, (q + nchip - 1) % nchip

    y, z, ny = q // nz, q % nz, nchip // nz

    def shift(i):
        j = i // nz
        return j + j // 2 * (1 - 2 * (j % 2))

    def chip_at(i, sign):
        kz, ky = i // ny, i % ny
        dz = nz // 2 + (kz + 1) // 2 * (1 - 2 * (kz % 2))
        dy = ny // 2 + (ky + 1) // 2 * (1 - 2 * (ky % 2))
        return lax.rem(y + ny + sign * dy, ny) * nz + lax.rem(z + nz + sign * dz, nz)

    def met(i, sign):
        return chip_at(i, sign) * CORES + c, lax.rem(x + ngrp + sign * shift(i), ngrp)

    loads = [pltpu.make_async_copy(bins_in, bins, in_sem.at[0]), pltpu.make_async_copy(mot_in, mot, in_sem.at[1]),
             pltpu.make_async_copy(pos_in, pos, in_sem.at[2]), pltpu.make_async_copy(vol_in, vols.at[me], in_sem.at[3]),
             pltpu.make_async_copy(infl_in, infl, in_sem.at[4])]
    for load in loads:
        load.start()

    barrier = pltpu.get_barrier_semaphore()

    def greet(device):
        pl.semaphore_signal(barrier, inc=1, device_id=device, device_id_type=MESH)

    for i in range(nchip):
        greet(met(i, -1))
    greet((up * CORES + c, x))
    greet((down * CORES + c, x))
    for o in range(1, members):
        pc, px = peer_of(me, o, ngrp)
        greet((q * CORES + pc, px))

    loads[0].wait()
    slab_of = bins[...] // ngrp
    sub = lax.broadcasted_iota(jnp.int32, (nslab, LANES), 0)
    tri_r = lax.broadcasted_iota(jnp.int32, (LANES, 2 * LANES), 0)
    tri_c = lax.broadcasted_iota(jnp.int32, (LANES, 2 * LANES), 1)
    tri = jnp.where((tri_r <= tri_c), 1.0, 0.0).astype(BF16)
    carry = jnp.zeros((nslab, LANES), F32)
    fold = 2 * LANES // span
    column = lax.broadcasted_iota(jnp.int32, (LANES, LANES), 1).astype(F32)
    for k in range(blocks):
        trow = slab_of[k : k + 1, :]
        hit = trow == sub
        cum = dot(jnp.where(hit, 1.0, 0.0).astype(BF16), tri)
        rank = jnp.sum(jnp.where(hit, cum[:, :LANES] + carry, 0.0), axis=0, keepdims=True)
        carry = carry + cum[:, LANES:]
        dest = (trow % fold * span).astype(F32) + (rank - 1.0)
        wide = jnp.broadcast_to(dest, (LANES, LANES)).T
        one[k * LANES : (k + 1) * LANES, :] = jnp.concatenate(
            [jnp.where(wide == column + h * LANES, 1.0, 0.0) for h in range(2)], axis=1).astype(BF16)

    for load in loads[1:]:
        load.wait()
    lane = lax.broadcasted_iota(jnp.int32, (1, LANES), 1)
    row = jnp.where(lane == infl.shape[1], cnt[0], 0)
    for l in range(infl.shape[1]):
        row = jnp.where(lane == l, infl[0, l], row)
    lists[pl.ds(me, 1)] = row[None]

    whole = jnp.concatenate([mot[...], pos[...], jnp.zeros((16 - ROWS, mot.shape[1]), F32)], axis=0)
    xp[...] = jnp.concatenate(split3(whole), axis=0)

    def to_bin(i):
        slot = x * nz + i % nz
        return pltpu.make_async_remote_copy(
            src_ref=send.at[chip_at(i, 1)], dst_ref=win.at[1, slot], send_sem=a_send.at[i], recv_sem=a_recv.at[slot],
            device_id=met(i, 1), device_id_type=MESH)

    def group_of(j):
        return (x + ngrp - shift(j * nz)) % ngrp

    def forward(j, to):
        part = pl.ds(group_of(j) * nz, nz)
        return pltpu.make_async_remote_copy(
            src_ref=win.at[1, part], dst_ref=win.at[0 if to == 0 else 2, part],
            send_sem=f_send.at[to, j], recv_sem=f_recv.at[to, j],
            device_id=((up if to == 0 else down) * CORES + c, x), device_id_type=MESH)

    def forward_group(j, _):
        def arrived(k, _):
            s = group_of(j) * nz + k
            pltpu.make_async_remote_copy(
                src_ref=send.at[0], dst_ref=win.at[1, s], send_sem=a_send.at[0], recv_sem=a_recv.at[s],
                device_id=met(0, 1), device_id_type=MESH).wait_recv()
            return 0

        lax.fori_loop(0, nz, arrived, 0)
        forward(j, 0).start()
        forward(j, 1).start()
        return 0

    tiles = slab_of // fold
    ntile = nslab // fold
    rows = 4
    for k in range(blocks // rows):
        cols = slice(k * rows * LANES, (k + 1) * rows * LANES)
        mine = jnp.concatenate([tiles[k * rows + r : k * rows + r + 1, :] for r in range(rows)], axis=1)
        piece = xp[:, cols]
        kept = jnp.concatenate([jnp.where(mine == p, piece, 0.0) for p in range(ntile)], axis=0).astype(BF16)
        product = dot(kept, one[cols, :])
        acc[...] = product if k == 0 else acc[...] + product
    for p in range(ntile):
        full = acc[48 * p : 48 * p + 16] + acc[48 * p + 16 : 48 * p + 32] + acc[48 * p + 32 : 48 * p + 48]
        send[2 * p] = full[:ROWS, :LANES]
        send[2 * p + 1] = full[:ROWS, LANES:]

    pl.semaphore_wait(barrier, nchip + 2 + members - 1)
    for i in range(nchip):
        to_bin(i).start()
    for o in range(1, members):
        pc, px = peer_of(me, o, ngrp)
        for ref, s_sem, r_sem in ((vols, v_send, v_recv), (lists, l_send, l_recv)):
            pltpu.make_async_remote_copy(
                src_ref=ref.at[me], dst_ref=ref.at[me], send_sem=s_sem.at[o], recv_sem=r_sem.at[o],
                device_id=(q * CORES + pc, px), device_id_type=MESH).start()
    lax.fori_loop(0, ngrp, forward_group, 0)

    left = lax.broadcasted_iota(jnp.int32, (ROWS, LANES), 1) < span
    row8 = lax.broadcasted_iota(jnp.int32, (8, LANES), 0)

    def prepare(chip, g):
        for k in range(nz // 2):
            a = win[chip, g * nz + 2 * k]
            b = win[chip, g * nz + 2 * k + 1]
            pair = (jnp.where(left, a, pltpu.roll(b, span, 1)), jnp.where(left, pltpu.roll(a, span, 1), b))
            cols = slice(k * LANES, (k + 1) * LANES)
            for tt in range(CORES):
                n = (chip * CORES + tt) * ngrp + g
                upper = pair[tt][:8]
                lower = jnp.concatenate([pair[tt][8:], jnp.zeros((16 - ROWS, LANES), F32)], axis=0)
                m1, m2, _ = split3(jnp.where(row8 == 7, 1.0, upper))
                mt[n, :, cols] = jnp.concatenate([m1, m2], axis=0).astype(BF16)
                x2, yz2 = upper * upper, lower * lower
                norm = x2[7:8] + yz2[0:1] + yz2[1:2] + 0.01
                y = -2.0 * jnp.where(row8 == 7, upper, lower)
                y = jnp.where(row8 == 2, norm, jnp.where(row8 == 3, 1.0, y))
                y1, y2, y3 = split3(y)
                fs[n, :, cols] = jnp.concatenate([y1, y2, y3, y1, y2, y1], axis=0).astype(BF16)

    def prepare_own(g, _):
        prepare(1, g)
        return 0

    lax.fori_loop(0, ngrp, prepare_own, 0)

    def vol_copies(o):
        other = (me + members - o) % members
        pc, px = peer_of(me, o, ngrp)
        return [pltpu.make_async_remote_copy(
            src_ref=ref.at[me], dst_ref=ref.at[other], send_sem=s_sem.at[o], recv_sem=r_sem.at[o],
            device_id=(q * CORES + pc, px), device_id_type=MESH)
            for ref, s_sem, r_sem in ((vols, v_send, v_recv), (lists, l_send, l_recv))]

    for o in range(1, members):
        for copy in vol_copies(o):
            copy.wait_recv()

    def prepare_vol(j, _):
        v = vols[j]
        v2 = v * v
        norm = v2[0:1] + v2[1:2] + v2[2:3]
        ones = jnp.ones_like(norm)
        zero = jnp.zeros_like(norm)
        w1, w2, w3 = split3(jnp.concatenate([v[1:3], ones, norm, zero, zero, zero, v[0:1]], axis=0))
        fv[j] = jnp.concatenate([w1, w1, w1, w2, w2, w3], axis=0).astype(BF16)
        return 0

    lax.fori_loop(0, members, prepare_vol, 0)

    for i in range(nchip):
        to_bin(i).wait_send()
    for o in range(1, members):
        for copy in vol_copies(o):
            copy.wait_send()

    def arrived_near(j, _):
        for to in range(2):
            forward(j, to).wait_recv()
        prepare(0, group_of(j))
        prepare(2, group_of(j))
        return 0

    lax.fori_loop(0, ngrp, arrived_near, 0)

    for j in range(ngrp):
        for to in range(2):
            forward(j, to).wait_send()


def exchange(nchip, ngrp, pos, mot, bins, vol, infl, cnt):
    members = CORES * ngrp
    nvol = vol.shape[1]
    width = pos.shape[1]
    nbin = 3 * CORES * ngrp
    nodes = nchip // ngrp * LANES // CORES
    dma = pltpu.SemaphoreType.DMA
    return pl.pallas_call(
        functools.partial(exchange_kernel, nchip, ngrp),
        out_shape=(
            jax.ShapeDtypeStruct((nbin, DEPTH, nodes), BF16),
            jax.ShapeDtypeStruct((nbin, 16, nodes), BF16),
            jax.ShapeDtypeStruct((members, DEPTH, nvol), BF16),
            jax.ShapeDtypeStruct((members, 1, LANES), jnp.int32),
        ),
        in_specs=[HBM] * 5 + [SMEM],
        out_specs=(VMEM, VMEM, VMEM, VMEM),
        scratch_shapes=[
            pltpu.SMEM(infl.shape, jnp.int32),
            pltpu.VMEM(pos.shape, F32),
            pltpu.VMEM(mot.shape, F32),
            pltpu.VMEM(bins.shape, jnp.int32),
            pltpu.VMEM((members, 3, nvol), F32),
            pltpu.VMEM((48, width), F32),
            pltpu.VMEM((width, 2 * LANES), BF16),
            pltpu.VMEM((nchip // 2 * 48, 2 * LANES), F32),
            pltpu.VMEM((nchip, ROWS, LANES), F32),
            pltpu.VMEM((3, nchip, ROWS, LANES), F32),
            dma((5,)),
            dma((nchip,)), dma((nchip,)),
            dma((2, ngrp)), dma((2, ngrp)),
            dma((members,)), dma((members,)),
            dma((members,)), dma((members,)),
        ],
        compiler_params=pltpu.CompilerParams(collective_id=0, has_side_effects=True, vmem_limit_bytes=40 << 20),
    )(pos, mot, bins, vol, infl, cnt)


def blended(fs, mt, fv, ns, js):
    r2 = [dot(fs[n], fv[j], ((0,), (0,))) for n, j in zip(ns, js)]
    sums = []
    for n, d in zip(ns, r2):
        w = pltpu.reciprocal(d * d, approx=True)
        w1 = w.astype(BF16)
        w2 = (w - w1.astype(F32)).astype(BF16)
        m = mt[n]
        sums.append(dot(m, w1) + dot(m, w2))
    return sums


def blend_kernel(ngrp, lmax, lists, fs, mt, fv, part, acc, block_of, bin_of):
    q, _, x = place()
    members = fv.shape[0]
    base = (q - 1) * CORES * ngrp

    def block(j, filled):
        acc[j] = jnp.zeros(acc.shape[1:], F32)

        def entry(l, filled):
            block_of[filled] = j
            bin_of[filled] = lists[j, 0, l] - base
            return filled + 1

        return lax.fori_loop(jnp.where(j % ngrp == x, LATE, 0), lists[j, 0, lmax], entry, filled)

    total = lax.fori_loop(0, members, block, 0)

    def together(first, many):
        js = [block_of[first + k] for k in range(many)]
        ns = [bin_of[first + k] for k in range(many)]
        for j, more in zip(js, blended(fs, mt, fv, ns, js)):
            acc[j] += more

    def four(i, _):
        together(4 * i, 4)
        return 0

    def one(i, _):
        together(i, 1)
        return 0

    lax.fori_loop(0, total // 4, four, 0)
    lax.fori_loop(total // 4 * 4, total, one, 0)

    def close(j, _):
        part[j] = acc[j, :8] + acc[j, 8:]
        return 0

    lax.fori_loop(0, members, close, 0)


def blend(ngrp, lmax, lists, fs, mt, fv):
    members, _, nvol = fv.shape
    return pl.pallas_call(
        functools.partial(blend_kernel, ngrp, lmax),
        out_shape=jax.ShapeDtypeStruct((members, 8, nvol), F32),
        in_specs=[SMEM, VMEM, VMEM, VMEM],
        out_specs=VMEM,
        scratch_shapes=[
            pltpu.VMEM((members, 16, nvol), F32),
            pltpu.SMEM((members * lmax,), jnp.int32),
            pltpu.SMEM((members * lmax,), jnp.int32),
        ],
        compiler_params=pltpu.CompilerParams(vmem_limit_bytes=48 << 20),
    )(lists, fs, mt, fv)


def combine_kernel(ngrp, lists, fs, mt, fv, part, out, across, along, sums, c_send, c_recv, x_send, x_recv):
    q, c, x = place()
    base = (q - 1) * CORES * ngrp

    def late(j):
        ns = [jnp.clip(lists[j, 0, l] - base, 0, fs.shape[0] - 1) for l in range(LATE)]
        more = sum(blended(fs, mt, fv, ns, [j] * LATE))
        return part[j] + (more[:8] + more[8:])

    barrier = pltpu.get_barrier_semaphore()
    there = (q * CORES + 1 - c, x)
    pl.semaphore_signal(barrier, inc=1, device_id=there, device_id_type=MESH)
    for o in range(1, ngrp):
        pl.semaphore_signal(barrier, inc=1, device_id=(q * CORES + c, (x + o) % ngrp), device_id_type=MESH)
    pl.semaphore_wait(barrier, ngrp)

    def cross(to, src):
        copy = pltpu.make_async_remote_copy(
            src_ref=src, dst_ref=across.at[to], send_sem=c_send.at[to], recv_sem=c_recv.at[to],
            device_id=there, device_id_type=MESH)
        copy.start()
        return copy

    others = [(o, (x + o) % ngrp) for o in (2, 1, 3)]
    crossing = [cross(to, part.at[(1 - c) * ngrp + to]) for _, to in others]
    moving = []
    for (o, to), copy in zip(others, crossing):
        copy.wait_recv()
        sums[o] = part[c * ngrp + to] + across[to]
        step = pltpu.make_async_remote_copy(
            src_ref=sums.at[o], dst_ref=along.at[o], send_sem=x_send.at[o], recv_sem=x_recv.at[o],
            device_id=(q * CORES + c, to), device_id_type=MESH)
        step.start()
        moving.append((o, step))

    sums[0] = late((1 - c) * ngrp + x)
    last = cross(x, sums.at[0])
    total = late(c * ngrp + x)
    for o, step in moving:
        step.wait_recv()
        total = total + along[o]
    last.wait_recv()
    total = total + across[x]
    out[...] = total[:7] / total[7:8]
    for copy in crossing + [last]:
        copy.wait_send()
    for _, step in moving:
        step.wait_send()


def combine(ngrp, lists, fs, mt, fv, part):
    nvol = part.shape[2]
    return pl.pallas_call(
        functools.partial(combine_kernel, ngrp),
        out_shape=jax.ShapeDtypeStruct((7, nvol), F32),
        in_specs=[SMEM] + [VMEM] * 4,
        out_specs=VMEM,
        scratch_shapes=[pltpu.VMEM((ngrp, 8, nvol), F32)] * 3 + [pltpu.SemaphoreType.DMA((ngrp,))] * 4,
        compiler_params=pltpu.CompilerParams(collective_id=1, has_side_effects=True, vmem_limit_bytes=48 << 20),
    )(lists, fs, mt, fv, part)


def on_device(surf_pos, surf_motion, surf_bin, vol_pos, influence, list_count):
    nchip = lax.axis_size("slab") // CORES
    ngrp = lax.axis_size("grp")
    bins = surf_bin.reshape(-1, LANES)
    surf_pos, surf_motion, bins, vol_pos, influence = (
        pltpu.with_memory_space_constraint(a, pltpu.HBM) for a in (surf_pos, surf_motion, bins, vol_pos, influence))
    fs, mt, fv, lists = exchange(nchip, ngrp, surf_pos, surf_motion, bins, vol_pos, influence, list_count)
    part = blend(ngrp, influence.shape[1], lists, fs, mt, fv)
    return combine(ngrp, lists, fs, mt, fv, part)


def solution(mesh):
    return jax.shard_map(
        on_device,
        mesh=mesh,
        in_specs=(
            P(None, ("slab", "grp")),
            P(None, ("slab", "grp")),
            P(("slab", "grp")),
            P(None, ("slab", "grp")),
            P(("slab", "grp"), None),
            P(("slab", "grp")),
        ),
        out_specs=P(None, ("slab", "grp")),
        check_vma=False,
    )
```
